32 devices in a mesh: groups: 2 (over y), leaf: 8 (over z, x), probe: 2 (over core).
Axes of the slice: x: 2, y: 2, z: 4, core: 2. Of those that a mesh axis runs over, the one named last changes fastest.
Arguments:
- rhs: float32 [16, 32768], P('probe', ('groups', 'leaf')), parts along dimension 1, may hold values from -6 to 6
- points: float32 [3, 32768], P(None, ('groups', 'leaf')), parts along dimension 1, may hold values from 0 to 4, as said below
- basis: bfloat16 [320, 32768], P(None, ('groups', 'leaf')), parts along dimension 1
- tree_order: int32 [32768], P(('groups', 'leaf')), parts along dimension 0, may hold values from 0 to 16383, as said below
- lengthscale: float32 [2], P('groups'), parts along dimension 0, may hold values from 0.1 to 0.8
Outputs:
- solution: float32 [16, 32768], P('probe', ('groups', 'leaf')), parts along dimension 1
- residual: float32 [16, 32768], P('probe', ('groups', 'leaf')), parts along dimension 1
The draws below stay inside these ranges and needn't reach their ends.
There are 2 independent parts, one for each index of `groups`. The reference program is written for one: setup_inputs(seed, part) draws one part's arguments, and reference() takes and returns one part's arrays. A program takes and returns all parts, laid end to end along the dimension named above; each array names one. Nothing has to cross between parts.
Inputs may be any that keep to these rules, and one draw needn't show every extreme that they name: `tree_order`: each block of 512 consecutive positions holds a permutation of that block's own positions. The 512 points of one leaf block lie in one unit cube.
All inputs are finite; a program needn't handle non-finite values.
Results may differ from the reference program's by a relative error of at most 0.034.
The reference program's roundings to bfloat16 on the way count: a program that leaves them out, or rounds other values in their place, can miss the bound.
Values sent between devices are 32-bit elements; how exact they have to be, the bound alone decides.
A program may use at most 64 MiB of HBM per device.

```python
import math
import jax
import jax.numpy as jnp
from jax import lax

LEAF = 512
K = 64
R = 16
ITERS = 4
LEVELS = 5
NPTS = 16384


LEVEL_GAIN = 8.0


SHARED_WEIGHT = 0.6


OWN_WEIGHT = 0.8


def shared_fields(key):
    return jax.random.truncated_normal(jax.random.fold_in(key, 5), -4.0, 4.0, (R, NPTS), jnp.float32)


def tree_permutation(key):
    order_key = jax.random.fold_in(key, 37)
    leaf_count = NPTS // LEAF
    leaf_keys = jax.random.split(order_key, leaf_count)
    orders = jax.vmap(lambda single: jax.random.permutation(single, LEAF))(leaf_keys)
    starts = (jnp.arange(leaf_count, dtype=jnp.int32) * LEAF)[:, None]
    return (orders.astype(jnp.int32) + starts).reshape(NPTS)


def draw_rhs(key, part):
    shared = shared_fields(key)
    order = tree_permutation(key)
    key = jax.random.fold_in(key, 41)
    own = jax.random.truncated_normal(key, -4.0, 4.0, (R, NPTS), jnp.float32)
    placed = jnp.zeros((R, NPTS), jnp.float32).at[:, order].set(shared)
    return SHARED_WEIGHT * placed + OWN_WEIGHT * own


def draw_points(key, part):
    key = jax.random.fold_in(key, 11)
    leaf_ids = jnp.arange(NPTS, dtype=jnp.int32) // LEAF
    corners = [jnp.zeros((NPTS,), jnp.int32), jnp.zeros((NPTS,), jnp.int32), jnp.zeros((NPTS,), jnp.int32)]
    for depth_step in range(LEVELS):
        halves = jnp.right_shift(leaf_ids, LEVELS - 1 - depth_step) % 2
        corner_axis = depth_step % 3
        corners[corner_axis] = corners[corner_axis] * 2 + halves
    anchor = jnp.stack(corners).astype(jnp.float32)
    offset = jax.random.uniform(key, (3, NPTS), jnp.float32)
    return anchor + offset


def draw_basis(key, part):
    shared = shared_fields(key)
    key = jax.random.fold_in(key, 23)
    depths = jnp.arange(LEVELS * K, dtype=jnp.int32) // K
    node_size = jnp.right_shift(jnp.int32(NPTS), depths).astype(jnp.float32)
    row_scale = jnp.sqrt(LEVEL_GAIN / node_size)[:, None]
    values = jax.random.truncated_normal(key, -4.0, 4.0, (LEVELS * K, NPTS), jnp.float32)
    values = values.at[:R].set(shared)
    return (values * row_scale).astype(jnp.bfloat16)


def draw_tree_order(key, part):
    return tree_permutation(key)


def setup_inputs(seed: int = 0, part: int = 0) -> dict:
    key_of = jax.random.split(jax.random.key(seed), 6)
    part_keys = jax.random.split(jax.random.fold_in(key_of[5], part), 6)
    rhs = draw_rhs(jax.random.fold_in(jax.random.fold_in(key_of[5], part), 71), part)
    points = draw_points(jax.random.fold_in(jax.random.fold_in(key_of[5], part), 71), part)
    basis = draw_basis(jax.random.fold_in(jax.random.fold_in(key_of[5], part), 71), part)
    tree_order = draw_tree_order(jax.random.fold_in(jax.random.fold_in(key_of[5], part), 71), part)
    lengthscale = jnp.clip(jnp.exp(jax.random.uniform(part_keys[4], (1,), jnp.float32, math.log(0.1), math.log(0.8))), 0.1, 0.8)
    return dict(rhs=rhs, points=points, basis=basis, tree_order=tree_order, lengthscale=lengthscale)


NOISE = 0.5
ROOT_THREE = 1.7320508

def leaf_tile(coords, scale):
    offsets = coords[:, :, None] - coords[:, None, :]
    distance = jnp.sqrt(lax.optimization_barrier(jnp.sum(offsets * offsets, axis=0)))
    scaled = ROOT_THREE * distance / scale
    return ((1.0 + scaled) * jnp.exp(-scaled)).astype(jnp.bfloat16)

def operate(vector, points, basis, scale):
    count = NPTS // LEAF
    low16 = vector.astype(jnp.bfloat16)
    blocks = jnp.transpose(low16.reshape(R, count, LEAF), (1, 0, 2))
    coords = jnp.transpose(points.reshape(3, count, LEAF), (1, 0, 2))

    def one_leaf(item):
        where, block = item
        return jnp.dot(block, leaf_tile(where, scale), preferred_element_type=jnp.float32)
    near = lax.map(one_leaf, (coords, blocks))
    result = jnp.transpose(near, (1, 0, 2)).reshape(R, NPTS) + NOISE * vector
    wide = low16.astype(jnp.float32)
    for depth in range(LEVELS):
        nodes = 2 ** depth
        factor = basis[depth * K:(depth + 1) * K].astype(jnp.float32).reshape(K, nodes, NPTS // nodes)
        pieces = wide.reshape(R, nodes, NPTS // nodes)
        node_sums = jnp.einsum('rmn,kmn->rmk', pieces, factor)
        node_low = node_sums.astype(jnp.bfloat16).astype(jnp.float32)
        result = result + jnp.einsum('rmk,kmn->rmn', node_low, factor).reshape(R, NPTS)
    return result

def reference(rhs, points, basis, tree_order, lengthscale):
    scale = lengthscale[0]
    right = jnp.take(rhs, tree_order, axis=1)
    iterate = jnp.zeros_like(right)
    remain = right
    direction = right
    norm_now = lax.optimization_barrier(jnp.sum(remain * remain, axis=1, keepdims=True))
    for iteration in range(ITERS):
        image = operate(direction, points, basis, scale)
        alpha = norm_now / lax.optimization_barrier(jnp.sum(direction * image, axis=1, keepdims=True))
        iterate = iterate + alpha * direction
        remain = remain - alpha * image
        norm_next = lax.optimization_barrier(jnp.sum(remain * remain, axis=1, keepdims=True))
        direction = remain + norm_next / norm_now * direction
        norm_now = norm_next
    solution = jnp.zeros_like(iterate).at[:, tree_order].set(iterate)
    residual = jnp.zeros_like(remain).at[:, tree_order].set(remain)
    return (solution, residual)
```

```python
import functools

import jax
import jax.numpy as jnp
from jax import lax
from jax.experimental import pallas as pl
from jax.experimental.pallas import tpu as pltpu
from jax.sharding import PartitionSpec as P

LEAF = 512
K = 64
ITERS = 4
CHUNK = 128

NOISE = 0.5
ROOT_THREE = 1.7320508
F32 = jnp.float32
BF16 = jnp.bfloat16
NN = (((1,), (0,)), ((), ()))
NT = (((1,), (1,)), ((), ()))


def dot(a, b, dims=NN):
    return lax.dot_general(a, b, dims, preferred_element_type=F32)


def split3(x):
    hi = x.astype(BF16)
    rest = x - hi.astype(F32)
    mid = rest.astype(BF16)
    low = (rest - mid.astype(F32)).astype(BF16)
    return jnp.concatenate([hi.astype(F32), mid.astype(F32), low.astype(F32)], axis=0).astype(BF16)


def join3(y):
    rows = y.shape[0] // 3
    return y[:rows] + (y[rows : 2 * rows] + y[2 * rows :])


def tree_levels(leaves):
    levels = [leaves]
    while len(levels[-1]) > 1:
        last = levels[-1]
        levels.append([last[2 * i] + last[2 * i + 1] for i in range(len(last) // 2)])
    return levels


def cg_kernel(
    n,
    cross,
    total,
    rhs_ref,
    points_ref,
    basis_ref,
    order_ref,
    scale_ref,
    solution_ref,
    residual_ref,
    tiles,
    picks,
    sums,
    scalars,
    send_sem,
    recv_sem,
):
    me = lax.axis_index("leaf")
    rows, span = rhs_ref.shape
    count = span // LEAF
    upper = cross * K
    width = sums.shape[-1]

    def partner(slot):
        other = me
        for b in range(cross):
            bit = (slot // 2**b) % 2
            mine = (me // 2**b) % 2
            other = other + bit * (1 - 2 * mine) * 2**b
        return other

    def each_partner(act):
        if n <= 8:
            for slot in range(1, n):
                act(slot)
        else:
            def step(slot, carry):
                act(slot)
                return carry
            lax.fori_loop(1, n, step, 0)

    def broadcast(buffer, at, sem):
        def act(slot):
            pltpu.make_async_remote_copy(
                src_ref=buffer.at[at, 0],
                dst_ref=buffer.at[at, slot],
                send_sem=send_sem.at[sem],
                recv_sem=recv_sem.at[sem],
                device_id={"leaf": partner(slot)},
                device_id_type=pl.DeviceIdType.MESH,
            ).start()
        each_partner(act)

    def arrived(buffer, at, sem):
        landed = buffer.at[at, pl.ds(1, n - 1)]
        pltpu.make_async_copy(landed, landed, recv_sem.at[sem]).wait()

    def left(buffer, at, sem):
        landed = buffer.at[at, pl.ds(1, n - 1)]
        pltpu.make_async_copy(landed, landed, send_sem.at[sem]).wait()

    barrier = pltpu.get_barrier_semaphore()

    def greet(slot):
        pl.semaphore_signal(
            barrier, inc=1, device_id={"leaf": partner(slot)}, device_id_type=pl.DeviceIdType.MESH
        )

    each_partner(greet)

    row_id = lax.broadcasted_iota(jnp.int32, (LEAF, LEAF), 0)
    right_parts = []
    for t in range(count):
        cols = slice(t * LEAF, (t + 1) * LEAF)
        wanted = order_ref[:, cols] % LEAF
        picks[t] = jnp.where(row_id == wanted, 1.0, 0.0).astype(BF16)
        right_parts.append(join3(dot(split3(rhs_ref[:, cols]), picks[t])))
    right = jnp.concatenate(right_parts, axis=1)

    def project_and_send(direction, it):
        low16 = direction.astype(BF16)
        wide = low16.astype(F32)
        both = jnp.concatenate([wide, direction - wide], axis=0).astype(BF16)
        sums[it, 0, :, :upper] = dot(both, basis_ref[:upper, :], NT)
        if it == 0:
            pl.semaphore_wait(barrier, n - 1)
        broadcast(sums, it, it)
        return low16

    low16 = project_and_send(right, 0)

    factor = ROOT_THREE / scale_ref[0]
    for t in range(count):
        cols = slice(t * LEAF, (t + 1) * LEAF)
        coords = points_ref[:, cols] * factor
        tall = jnp.transpose(
            jnp.concatenate([coords, jnp.zeros((5, LEAF), F32)], axis=0)
        )
        for c in range(LEAF // CHUNK):
            part = slice(c * CHUNK, (c + 1) * CHUNK)
            square = None
            for axis in range(3):
                offset = tall[part, axis : axis + 1] - coords[axis : axis + 1, :]
                term = offset * offset
                square = term if square is None else square + term
            scaled = jnp.sqrt(square)
            tiles[t, part, :] = ((1.0 + scaled) * jnp.exp(-scaled)).astype(BF16)

    lane = lax.broadcasted_iota(jnp.int32, (rows, width), 1)
    halves = 2 ** (total - cross - 1)
    half = span // halves
    lane128 = lax.broadcasted_iota(jnp.int32, (rows, 128), 1)

    iterate = jnp.zeros_like(right)
    remain = right
    direction = right
    norm_now = None
    for it in range(ITERS):
        near = jnp.concatenate(
            [dot(low16[:, t * LEAF : (t + 1) * LEAF], tiles[t]) for t in range(count)], axis=1
        )
        local = [
            dot(low16[:, h * half : (h + 1) * half], basis_ref[upper:, h * half : (h + 1) * half], NT)
            for h in range(halves)
        ]
        spread = []
        for h in range(halves):
            cuts = []
            for depth in range(total - cross):
                size = halves // 2**depth
                first = h // size * size
                whole = local[first]
                for other in range(first + 1, first + size):
                    whole = whole + local[other]
                cuts.append(whole[:, depth * K : (depth + 1) * K])
            node = jnp.concatenate(cuts, axis=1).astype(BF16)
            spread.append(dot(node, basis_ref[upper:, h * half : (h + 1) * half]))
        result = near + NOISE * direction + jnp.concatenate(spread, axis=1)
        mine = jnp.sum(direction * result, axis=1, keepdims=True)
        if it == 0:
            first_norm = jnp.sum(remain * remain, axis=1, keepdims=True)
            scalars[it, 0] = jnp.where(lane128 < 64, mine, first_norm)
        else:
            scalars[it, 0] = jnp.broadcast_to(mine, (rows, 128))
        broadcast(scalars, it, ITERS + it)

        arrived(sums, it, it)
        levels = tree_levels([sums[it, j] for j in range(n)])
        node = jnp.zeros((rows, width), F32)
        cover = jnp.zeros((rows, width), F32)
        for depth in range(cross):
            here = (lane >= depth * K) & (lane < (depth + 1) * K)
            nodes = levels[cross - depth]
            node = jnp.where(here, nodes[0][:rows], node)
            terms = [s[:rows].astype(BF16).astype(F32) * (s[:rows] + s[rows:]) for s in nodes]
            cover = jnp.where(here, tree_levels(terms)[-1][0], cover)
        result = result + dot(node[:, :upper].astype(BF16), basis_ref[:upper, :])
        cover = jnp.sum(cover, axis=1, keepdims=True)

        arrived(scalars, it, ITERS + it)
        gathered = tree_levels([scalars[it, j] for j in range(n)])[-1][0]
        curve = gathered[:, :1] + cover
        if it == 0:
            norm_now = gathered[:, 64:65]
        alpha = norm_now / curve
        remain = remain - alpha * result
        if it + 1 < ITERS:
            at = ITERS + it
            scalars[at, 0] = jnp.broadcast_to(
                jnp.sum(remain * remain, axis=1, keepdims=True), (rows, 128)
            )
            broadcast(scalars, at, ITERS + at)
            iterate = iterate + alpha * direction
            arrived(scalars, at, ITERS + at)
            norm_next = tree_levels([scalars[at, j] for j in range(n)])[-1][0][:, :1]
            direction = remain + norm_next / norm_now * direction
            norm_now = norm_next
            low16 = project_and_send(direction, it + 1)
        else:
            iterate = iterate + alpha * direction

    for t in range(count):
        cols = slice(t * LEAF, (t + 1) * LEAF)
        both = jnp.concatenate([iterate[:, cols], remain[:, cols]], axis=0)
        placed = join3(dot(split3(both), picks[t], NT))
        solution_ref[:, cols] = placed[:rows]
        residual_ref[:, cols] = placed[rows:]
    for it in range(ITERS):
        left(sums, it, it)
    for at in range(2 * ITERS - 1):
        left(scalars, at, ITERS + at)


def body(rhs, points, basis, tree_order, lengthscale):
    rows, span = rhs.shape
    n = lax.axis_size("leaf")
    cross = n.bit_length() - 1
    total = basis.shape[0] // K
    width = -(-cross * K // 128) * 128
    vmem = pl.BlockSpec(memory_space=pltpu.VMEM)
    rounds = 3 * ITERS - 1
    return pl.pallas_call(
        functools.partial(cg_kernel, n, cross, total),
        out_shape=[jax.ShapeDtypeStruct((rows, span), F32)] * 2,
        in_specs=[vmem, vmem, vmem, vmem, pl.BlockSpec(memory_space=pltpu.SMEM)],
        out_specs=[vmem, vmem],
        scratch_shapes=[
            pltpu.VMEM((span // LEAF, LEAF, LEAF), BF16),
            pltpu.VMEM((span // LEAF, LEAF, LEAF), BF16),
            pltpu.VMEM((ITERS, n, 2 * rows, width), F32),
            pltpu.VMEM((2 * ITERS - 1, n, rows, 128), F32),
            pltpu.SemaphoreType.DMA((rounds,)),
            pltpu.SemaphoreType.DMA((rounds,)),
        ],
        compiler_params=pltpu.CompilerParams(
            collective_id=0, has_side_effects=True, vmem_limit_bytes=48 * 2**20
        ),
        name="cg",
    )(rhs, points, basis, tree_order.reshape(1, span), lengthscale)


def solution(mesh):
    in_specs = (
        P("probe", ("groups", "leaf")),
        P(None, ("groups", "leaf")),
        P(None, ("groups", "leaf")),
        P(("groups", "leaf")),
        P("groups"),
    )
    out_specs = (P("probe", ("groups", "leaf")), P("probe", ("groups", "leaf")))
    return jax.shard_map(body, mesh=mesh, in_specs=in_specs, out_specs=out_specs, check_vma=False)
```

```python
import functools

import jax
import jax.numpy as jnp
from jax import lax
from jax.experimental import pallas as pl
from jax.experimental.pallas import tpu as pltpu
from jax.sharding import PartitionSpec as P

LEAF = 512
K = 64
ITERS = 4
CHUNK = 128

NOISE = 0.5
ROOT_THREE = 1.7320508
F32 = jnp.float32
BF16 = jnp.bfloat16
NN = (((1,), (0,)), ((), ()))
NT = (((1,), (1,)), ((), ()))


def dot(a, b, dims=NN):
    return lax.dot_general(a, b, dims, preferred_element_type=F32)


def split3(x):
    hi = x.astype(BF16)
    rest = x - hi.astype(F32)
    mid = rest.astype(BF16)
    low = (rest - mid.astype(F32)).astype(BF16)
    return jnp.concatenate([hi.astype(F32), mid.astype(F32), low.astype(F32)], axis=0).astype(BF16)


def join3(y):
    rows = y.shape[0] // 3
    return y[:rows] + (y[rows : 2 * rows] + y[2 * rows :])


def tree_levels(leaves):
    levels = [leaves]
    while len(levels[-1]) > 1:
        last = levels[-1]
        levels.append([last[2 * i] + last[2 * i + 1] for i in range(len(last) // 2)])
    return levels


def cg_kernel(
    n,
    cross,
    total,
    rhs_ref,
    points_ref,
    basis_ref,
    order_ref,
    scale_ref,
    solution_ref,
    residual_ref,
    tiles,
    picks,
    sums,
    scalars,
    gram,
    forms,
    send_sem,
    recv_sem,
):
    me = lax.axis_index("leaf")
    core = lax.axis_index("probe")
    fused = gram is not None
    rows, span = rhs_ref.shape
    count = span // LEAF
    upper = cross * K
    width = sums.shape[-1]

    def partner(slot):
        other = me
        for b in range(cross):
            bit = (slot // 2**b) % 2
            mine = (me // 2**b) % 2
            other = other + bit * (1 - 2 * mine) * 2**b
        return other

    def each_partner(act):
        if n <= 8:
            for slot in range(1, n):
                act(slot)
        else:
            def step(slot, carry):
                act(slot)
                return carry
            lax.fori_loop(1, n, step, 0)

    def broadcast(buffer, at, sem):
        def act(slot):
            pltpu.make_async_remote_copy(
                src_ref=buffer.at[at, 0],
                dst_ref=buffer.at[at, slot],
                send_sem=send_sem.at[sem],
                recv_sem=recv_sem.at[sem],
                device_id={"leaf": partner(slot)},
                device_id_type=pl.DeviceIdType.MESH,
            ).start()
        each_partner(act)

    def arrived(buffer, at, sem):
        landed = buffer.at[at, pl.ds(1, n - 1)]
        pltpu.make_async_copy(landed, landed, recv_sem.at[sem]).wait()

    def left(buffer, at, sem):
        landed = buffer.at[at, pl.ds(1, n - 1)]
        pltpu.make_async_copy(landed, landed, send_sem.at[sem]).wait()

    barrier = pltpu.get_barrier_semaphore()

    def greet(slot):
        pl.semaphore_signal(
            barrier, inc=1, device_id={"leaf": partner(slot)}, device_id_type=pl.DeviceIdType.MESH
        )

    each_partner(greet)
    if fused:
        pl.semaphore_signal(
            barrier, inc=1, device_id={"probe": 1 - core}, device_id_type=pl.DeviceIdType.MESH
        )

    row_id = lax.broadcasted_iota(jnp.int32, (LEAF, LEAF), 0)
    right_parts = []
    for t in range(count):
        cols = slice(t * LEAF, (t + 1) * LEAF)
        wanted = order_ref[:, cols] % LEAF
        picks[t] = jnp.where(row_id == wanted, 1.0, 0.0).astype(BF16)
        right_parts.append(join3(dot(split3(rhs_ref[:, cols]), picks[t])))
    right = jnp.concatenate(right_parts, axis=1)

    def project_and_send(direction, it):
        low16 = direction.astype(BF16)
        wide = low16.astype(F32)
        both = jnp.concatenate([wide, direction - wide], axis=0).astype(BF16)
        sums[it, 0, :, :upper] = dot(both, basis_ref[:upper, :], NT)
        if it == 0:
            pl.semaphore_wait(barrier, n if fused else n - 1)
        broadcast(sums, it, it)
        return low16

    low16 = project_and_send(right, 0)

    def swap(sem):
        return pltpu.make_async_remote_copy(
            src_ref=gram.at[core, pl.ds(1, n - 1)],
            dst_ref=gram.at[core, pl.ds(1, n - 1)],
            send_sem=send_sem.at[sem],
            recv_sem=recv_sem.at[sem],
            device_id={"probe": 1 - core},
            device_id_type=pl.DeviceIdType.MESH,
        )

    gram_sem, swap_sem = 2 * ITERS, 2 * ITERS + 1
    if fused:
        square = dot(basis_ref[:upper, :], basis_ref[:upper, :], NT)
        first = square[:K, :]
        second = jnp.concatenate([square[K : 2 * K, K:], square[2 * K :, 2 * K :]], axis=1)
        for h, block in enumerate((first, second)):
            gram[h, 0, :K, :] = block[:, :128]
            gram[h, 0, K:, :] = jnp.concatenate([block[: K // 2, 128:], block[K // 2 :, 128:]], axis=1)
        for slot in range(1, n):
            pltpu.make_async_remote_copy(
                src_ref=gram.at[core, 0],
                dst_ref=gram.at[core, slot],
                send_sem=send_sem.at[gram_sem],
                recv_sem=recv_sem.at[gram_sem],
                device_id={"leaf": partner(slot)},
                device_id_type=pl.DeviceIdType.MESH,
            ).start()

    def build_forms():
        pairs = []
        for p in range(n // 2):
            rows_of = []
            for h in range(2):
                packed = gram[h, 2 * p] + gram[h, 2 * p + 1]
                tail = jnp.concatenate([packed[K:, :K], packed[K:, K:]], axis=0)
                rows_of.append(jnp.concatenate([packed[:K], tail], axis=1))
            pairs.append(rows_of)
        top = functools.reduce(jnp.maximum, [jnp.abs(block) for blocks in pairs for block in blocks])
        top = jnp.max(jnp.max(top, axis=1, keepdims=True), axis=0, keepdims=True)
        top = jnp.maximum(top, 1e-30)
        turn = 1.0 / top
        lane_k = lax.broadcasted_iota(jnp.int32, (K, upper), 1)
        for p, (a, b) in enumerate(pairs):
            none = jnp.zeros((K, K), F32)
            grid = [
                jnp.where(lane_k < K, a, 2.0 * a),
                jnp.concatenate([none, b[:, :K], 2.0 * b[:, K : 2 * K]], axis=1),
                jnp.concatenate([none, none, b[:, 2 * K :]], axis=1),
            ]
            whole = jnp.concatenate(grid, axis=0) * turn
            hi = whole.astype(BF16)
            rest = whole - hi.astype(F32)
            mid = rest.astype(BF16)
            low = (rest - mid.astype(F32)).astype(BF16)
            forms[p, 0] = hi
            forms[p, 1] = mid
            forms[p, 2] = low
        return top

    factor = ROOT_THREE / scale_ref[0]
    for t in range(count):
        cols = slice(t * LEAF, (t + 1) * LEAF)
        coords = points_ref[:, cols] * factor
        tall = jnp.transpose(
            jnp.concatenate([coords, jnp.zeros((5, LEAF), F32)], axis=0)
        )
        for c in range(LEAF // CHUNK):
            part = slice(c * CHUNK, (c + 1) * CHUNK)
            square = None
            for axis in range(3):
                offset = tall[part, axis : axis + 1] - coords[axis : axis + 1, :]
                term = offset * offset
                square = term if square is None else square + term
            scaled = jnp.sqrt(square)
            tiles[t, part, :] = ((1.0 + scaled) * jnp.exp(-scaled)).astype(BF16)

    lane = lax.broadcasted_iota(jnp.int32, (rows, width), 1)
    halves = 2 ** (total - cross - 1)
    half = span // halves
    lane128 = lax.broadcasted_iota(jnp.int32, (rows, 128), 1)

    iterate = jnp.zeros_like(right)
    remain = right
    direction = right
    norm_now = None
    for it in range(ITERS):
        near = jnp.concatenate(
            [dot(low16[:, t * LEAF : (t + 1) * LEAF], tiles[t]) for t in range(count)], axis=1
        )
        local = [
            dot(low16[:, h * half : (h + 1) * half], basis_ref[upper:, h * half : (h + 1) * half], NT)
            for h in range(halves)
        ]
        spread = []
        for h in range(halves):
            cuts = []
            for depth in range(total - cross):
                size = halves // 2**depth
                first = h // size * size
                whole = local[first]
                for other in range(first + 1, first + size):
                    whole = whole + local[other]
                cuts.append(whole[:, depth * K : (depth + 1) * K])
            node = jnp.concatenate(cuts, axis=1).astype(BF16)
            spread.append(dot(node, basis_ref[upper:, h * half : (h + 1) * half]))
        result = near + NOISE * direction + jnp.concatenate(spread, axis=1)
        mine = jnp.sum(direction * result, axis=1, keepdims=True)
        more = it + 1 < ITERS
        if fused:
            parts = [mine, jnp.sum(remain * remain, axis=1, keepdims=True)]
            message = jnp.zeros((rows, width), F32)
            if more:
                if it == 0:
                    size = jnp.maximum(jnp.max(jnp.abs(result), axis=1, keepdims=True), 1e-30)
                    shrink = 1.0 / size
                unit = result * shrink
                wide = unit.astype(BF16).astype(F32)
                both = jnp.concatenate([wide, unit - wide], axis=0).astype(BF16)
                seen = dot(both, basis_ref[:upper, :], NT)
                seen = seen[:rows] + seen[rows:]
                message = jnp.concatenate([seen, jnp.zeros((rows, width - upper), F32)], axis=1)
                parts += [
                    jnp.sum(unit * unit, axis=1, keepdims=True),
                    mine if it == 0 else jnp.sum(remain * result, axis=1, keepdims=True),
                    size,
                ]
            for i, part in enumerate(parts):
                message = jnp.where(lane == upper + i, part, message)
            scalars[it, 0] = message
        elif it == 0:
            first_norm = jnp.sum(remain * remain, axis=1, keepdims=True)
            scalars[it, 0] = jnp.where(lane128 < 64, mine, first_norm)
        else:
            scalars[it, 0] = jnp.broadcast_to(mine, (rows, 128))
        broadcast(scalars, it, ITERS + it)
        if fused and it == 0:
            arrived_gram = gram.at[core, pl.ds(1, n - 1)]
            pltpu.make_async_copy(arrived_gram, arrived_gram, recv_sem.at[gram_sem]).wait()
            swap(swap_sem).start()

        arrived(sums, it, it)
        levels = tree_levels([sums[it, j] for j in range(n)])
        node = jnp.zeros((rows, width), F32)
        cover = jnp.zeros((rows, width), F32)
        for depth in range(cross):
            here = (lane >= depth * K) & (lane < (depth + 1) * K)
            nodes = levels[cross - depth]
            node = jnp.where(here, nodes[0][:rows], node)
            terms = [s[:rows].astype(BF16).astype(F32) * (s[:rows] + s[rows:]) for s in nodes]
            cover = jnp.where(here, tree_levels(terms)[-1][0], cover)
        result = result + dot(node[:, :upper].astype(BF16), basis_ref[:upper, :])
        cover = jnp.sum(cover, axis=1, keepdims=True)

        if fused:
            if more:
                chains, turned = [], []
                for p in range(n // 2):
                    chain = jnp.zeros((rows, width), F32)
                    full = jnp.zeros((rows, width), F32)
                    for depth in range(cross):
                        here = (lane >= depth * K) & (lane < (depth + 1) * K)
                        at = levels[cross - depth][p // 2 ** (cross - 1 - depth)]
                        chain = jnp.where(here, at[:rows].astype(BF16).astype(F32), chain)
                        if p % 2 ** (cross - 1 - depth) == 0:
                            full = jnp.where(here, at[:rows] + at[rows:], full)
                    chains.append(chain)
                    turned.append(full)
                if it == 0:
                    remain_cover = cover
                else:
                    moved = [now - ratio * old for now, old in zip(turned, turned_old)]
                    terms = [chain * there for chain, there in zip(chains, moved)]
                    remain_cover = jnp.sum(tree_levels(terms)[-1][0], axis=1, keepdims=True)
                turned_old = turned
                if it == 0:
                    swap(swap_sem).wait_recv()
                    form_top = build_forms()
                terms = []
                for p in range(n // 2):
                    chain16 = chains[p][:, :upper].astype(BF16)
                    image = dot(chain16, forms[p, 0]) + (
                        dot(chain16, forms[p, 1]) + dot(chain16, forms[p, 2])
                    )
                    terms.append(image * chains[p][:, :upper])
                form = jnp.sum(tree_levels(terms)[-1][0], axis=1, keepdims=True)

            arrived(scalars, it, ITERS + it)
            got = [scalars[it, j] for j in range(n)]
            gathered = tree_levels(got)[-1][0]
            curve = gathered[:, upper : upper + 1] + cover
            norm_now = gathered[:, upper + 1 : upper + 2]
            alpha = norm_now / curve
            if more:
                if it == 0:
                    sizes = [row[:, upper + 4 : upper + 5] for row in got]
                terms = []
                for j in range(n):
                    reach = alpha * sizes[j]
                    factors = jnp.where(
                        lane < upper,
                        (2.0 * alpha) * chains[j // 2],
                        jnp.where(lane == upper + 2, reach, 0.0),
                    )
                    terms.append(reach * (factors * got[j]))
                spent = jnp.sum(tree_levels(terms)[-1][0], axis=1, keepdims=True)
                crossed = alpha * (gathered[:, upper + 3 : upper + 4] + remain_cover)
                norm_next = (norm_now - 2.0 * crossed) + (spent + (alpha * form_top) * (alpha * form))
                ratio = norm_next / norm_now
            iterate = iterate + alpha * direction
            remain = remain - alpha * result
            if more:
                direction = remain + ratio * direction
                low16 = project_and_send(direction, it + 1)
            continue

        arrived(scalars, it, ITERS + it)
        gathered = tree_levels([scalars[it, j] for j in range(n)])[-1][0]
        curve = gathered[:, :1] + cover
        if it == 0:
            norm_now = gathered[:, 64:65]
        alpha = norm_now / curve
        remain = remain - alpha * result
        if it + 1 < ITERS:
            at = ITERS + it
            scalars[at, 0] = jnp.broadcast_to(
                jnp.sum(remain * remain, axis=1, keepdims=True), (rows, 128)
            )
            broadcast(scalars, at, ITERS + at)
            iterate = iterate + alpha * direction
            arrived(scalars, at, ITERS + at)
            norm_next = tree_levels([scalars[at, j] for j in range(n)])[-1][0][:, :1]
            direction = remain + norm_next / norm_now * direction
            norm_now = norm_next
            low16 = project_and_send(direction, it + 1)
        else:
            iterate = iterate + alpha * direction

    for t in range(count):
        cols = slice(t * LEAF, (t + 1) * LEAF)
        both = jnp.concatenate([iterate[:, cols], remain[:, cols]], axis=0)
        placed = join3(dot(split3(both), picks[t], NT))
        solution_ref[:, cols] = placed[:rows]
        residual_ref[:, cols] = placed[rows:]
    for it in range(ITERS):
        left(sums, it, it)
    for at in range(ITERS if fused else 2 * ITERS - 1):
        left(scalars, at, ITERS + at)
    if fused:
        sent = gram.at[core, pl.ds(1, n - 1)]
        pltpu.make_async_copy(sent, sent, send_sem.at[gram_sem]).wait()
        swap(swap_sem).wait_send()


def body(rhs, points, basis, tree_order, lengthscale):
    rows, span = rhs.shape
    n = lax.axis_size("leaf")
    cross = n.bit_length() - 1
    total = basis.shape[0] // K
    fused = n == 8
    width = -(-(cross * K + 64) // 128) * 128
    vmem = pl.BlockSpec(memory_space=pltpu.VMEM)
    rounds = 3 * ITERS - 1

    def kernel(*refs):
        if not fused:
            refs = refs[:11] + (None, None) + refs[11:]
        cg_kernel(n, cross, total, *refs)

    return pl.pallas_call(
        kernel,
        out_shape=[jax.ShapeDtypeStruct((rows, span), F32)] * 2,
        in_specs=[vmem, vmem, vmem, vmem, pl.BlockSpec(memory_space=pltpu.SMEM)],
        out_specs=[vmem, vmem],
        scratch_shapes=[shape for shape in [
            pltpu.VMEM((span // LEAF, LEAF, LEAF), BF16),
            pltpu.VMEM((span // LEAF, LEAF, LEAF), BF16),
            pltpu.VMEM((ITERS, n, 2 * rows, width), F32),
            pltpu.VMEM((ITERS, n, rows, width) if fused else (2 * ITERS - 1, n, rows, 128), F32),
            pltpu.VMEM((2, n, K * 3 // 2, 128), F32) if fused else None,
            pltpu.VMEM((n // 2, 3, cross * K, cross * K), BF16) if fused else None,
            pltpu.SemaphoreType.DMA((rounds,)),
            pltpu.SemaphoreType.DMA((rounds,)),
        ] if shape is not None],
        compiler_params=pltpu.CompilerParams(
            collective_id=0, has_side_effects=True, vmem_limit_bytes=48 * 2**20
        ),
        name="cg",
    )(rhs, points, basis, tree_order.reshape(1, span), lengthscale)


def solution(mesh):
    in_specs = (
        P("probe", ("groups", "leaf")),
        P(None, ("groups", "leaf")),
        P(None, ("groups", "leaf")),
        P(("groups", "leaf")),
        P("groups"),
    )
    out_specs = (P("probe", ("groups", "leaf")), P("probe", ("groups", "leaf")))
    return jax.shard_map(body, mesh=mesh, in_specs=in_specs, out_specs=out_specs, check_vma=False)
```

```python
import functools

import jax
import jax.numpy as jnp
from jax import lax
from jax.experimental import pallas as pl
from jax.experimental.pallas import tpu as pltpu
from jax.sharding import PartitionSpec as P

LEAF = 512
K = 64
ITERS = 4
CHUNK = 128

NOISE = 0.5
ROOT_THREE = 1.7320508
F32 = jnp.float32
BF16 = jnp.bfloat16
NN = (((1,), (0,)), ((), ()))
NT = (((1,), (1,)), ((), ()))


def dot(a, b, dims=NN):
    return lax.dot_general(a, b, dims, preferred_element_type=F32)


def split3(x):
    hi = x.astype(BF16)
    rest = x - hi.astype(F32)
    mid = rest.astype(BF16)
    low = (rest - mid.astype(F32)).astype(BF16)
    return jnp.concatenate([hi.astype(F32), mid.astype(F32), low.astype(F32)], axis=0).astype(BF16)


def join3(y):
    rows = y.shape[0] // 3
    return y[:rows] + (y[rows : 2 * rows] + y[2 * rows :])


def tree_levels(leaves):
    levels = [leaves]
    while len(levels[-1]) > 1:
        last = levels[-1]
        levels.append([last[2 * i] + last[2 * i + 1] for i in range(len(last) // 2)])
    return levels


def cg_kernel(
    n,
    cross,
    total,
    rhs_hbm,
    points_hbm,
    basis_hbm,
    order_hbm,
    scale_ref,
    solution_ref,
    residual_ref,
    tiles,
    picks,
    sums,
    scalars,
    gram,
    forms,
    rhs_ref,
    points_ref,
    basis_ref,
    order_ref,
    send_sem,
    recv_sem,
    load_sem,
):
    me = lax.axis_index("leaf")
    core = lax.axis_index("probe")
    fused = gram is not None
    rows, span = rhs_ref.shape
    count = span // LEAF
    upper = cross * K
    width = sums.shape[-1]

    def partner(slot):
        other = me
        for b in range(cross):
            bit = (slot // 2**b) % 2
            mine = (me // 2**b) % 2
            other = other + bit * (1 - 2 * mine) * 2**b
        return other

    def each_partner(act):
        if n <= 8:
            for slot in range(1, n):
                act(slot)
        else:
            def step(slot, carry):
                act(slot)
                return carry
            lax.fori_loop(1, n, step, 0)

    def broadcast(buffer, at, sem):
        def act(slot):
            pltpu.make_async_remote_copy(
                src_ref=buffer.at[at, 0],
                dst_ref=buffer.at[at, slot],
                send_sem=send_sem.at[sem],
                recv_sem=recv_sem.at[sem],
                device_id={"leaf": partner(slot)},
                device_id_type=pl.DeviceIdType.MESH,
            ).start()
        each_partner(act)

    def arrived(buffer, at, sem):
        landed = buffer.at[at, pl.ds(1, n - 1)]
        pltpu.make_async_copy(landed, landed, recv_sem.at[sem]).wait()

    def left(buffer, at, sem):
        landed = buffer.at[at, pl.ds(1, n - 1)]
        pltpu.make_async_copy(landed, landed, send_sem.at[sem]).wait()

    sources = (order_hbm, rhs_hbm, basis_hbm, points_hbm)
    targets = (order_ref, rhs_ref, basis_ref, points_ref)
    loads = [
        pltpu.make_async_copy(source, target, load_sem.at[i])
        for i, (source, target) in enumerate(zip(sources, targets))
    ]
    for load in loads:
        load.start()

    barrier = pltpu.get_barrier_semaphore()

    def greet(slot):
        pl.semaphore_signal(
            barrier, inc=1, device_id={"leaf": partner(slot)}, device_id_type=pl.DeviceIdType.MESH
        )

    each_partner(greet)
    if fused:
        pl.semaphore_signal(
            barrier, inc=1, device_id={"probe": 1 - core}, device_id_type=pl.DeviceIdType.MESH
        )

    loads[0].wait()
    loads[1].wait()
    row_id = lax.broadcasted_iota(jnp.int32, (LEAF, LEAF), 0)
    right_parts = []
    for t in range(count):
        cols = slice(t * LEAF, (t + 1) * LEAF)
        wanted = order_ref[:, cols] % LEAF
        picks[t] = jnp.where(row_id == wanted, 1.0, 0.0).astype(BF16)
        right_parts.append(join3(dot(split3(rhs_ref[:, cols]), picks[t])))
    right = jnp.concatenate(right_parts, axis=1)

    def project_and_send(direction, it):
        low16 = direction.astype(BF16)
        wide = low16.astype(F32)
        both = jnp.concatenate([wide, direction - wide], axis=0).astype(BF16)
        sums[it, 0, :, :upper] = dot(both, basis_ref[:upper, :], NT)
        if it == 0:
            pl.semaphore_wait(barrier, n if fused else n - 1)
        broadcast(sums, it, it)
        return low16

    loads[2].wait()
    low16 = project_and_send(right, 0)

    def swap(sem):
        return pltpu.make_async_remote_copy(
            src_ref=gram.at[core, pl.ds(1, n - 1)],
            dst_ref=gram.at[core, pl.ds(1, n - 1)],
            send_sem=send_sem.at[sem],
            recv_sem=recv_sem.at[sem],
            device_id={"probe": 1 - core},
            device_id_type=pl.DeviceIdType.MESH,
        )

    gram_sem, swap_sem = 2 * ITERS, 2 * ITERS + 1

    def send_gram():
        square = dot(basis_ref[:upper, :], basis_ref[:upper, :], NT)
        first = square[:K, :]
        second = jnp.concatenate([square[K : 2 * K, K:], square[2 * K :, 2 * K :]], axis=1)
        for h, block in enumerate((first, second)):
            gram[h, 0, :K, :] = block[:, :128]
            gram[h, 0, K:, :] = jnp.concatenate([block[: K // 2, 128:], block[K // 2 :, 128:]], axis=1)
        for slot in range(1, n):
            pltpu.make_async_remote_copy(
                src_ref=gram.at[core, 0],
                dst_ref=gram.at[core, slot],
                send_sem=send_sem.at[gram_sem],
                recv_sem=recv_sem.at[gram_sem],
                device_id={"leaf": partner(slot)},
                device_id_type=pl.DeviceIdType.MESH,
            ).start()

    def build_forms():
        pairs = []
        for p in range(n // 2):
            rows_of = []
            for h in range(2):
                packed = gram[h, 2 * p] + gram[h, 2 * p + 1]
                tail = jnp.concatenate([packed[K:, :K], packed[K:, K:]], axis=0)
                rows_of.append(jnp.concatenate([packed[:K], tail], axis=1))
            pairs.append(rows_of)
        top = functools.reduce(jnp.maximum, [jnp.abs(block) for blocks in pairs for block in blocks])
        top = jnp.max(jnp.max(top, axis=1, keepdims=True), axis=0, keepdims=True)
        top = jnp.maximum(top, 1e-30)
        turn = 1.0 / top
        lane_k = lax.broadcasted_iota(jnp.int32, (K, upper), 1)
        for p, (a, b) in enumerate(pairs):
            none = jnp.zeros((K, K), F32)
            grid = [
                jnp.where(lane_k < K, a, 2.0 * a),
                jnp.concatenate([none, b[:, :K], 2.0 * b[:, K : 2 * K]], axis=1),
                jnp.concatenate([none, none, b[:, 2 * K :]], axis=1),
            ]
            whole = jnp.concatenate(grid, axis=0) * turn
            hi = whole.astype(BF16)
            rest = whole - hi.astype(F32)
            mid = rest.astype(BF16)
            low = (rest - mid.astype(F32)).astype(BF16)
            forms[p, 0] = hi
            forms[p, 1] = mid
            forms[p, 2] = low
        return top

    loads[3].wait()
    factor = ROOT_THREE / scale_ref[0]
    for t in range(count):
        cols = slice(t * LEAF, (t + 1) * LEAF)
        coords = points_ref[:, cols] * factor
        tall = jnp.transpose(
            jnp.concatenate([coords, jnp.zeros((5, LEAF), F32)], axis=0)
        )
        for c in range(LEAF // CHUNK):
            part = slice(c * CHUNK, (c + 1) * CHUNK)
            square = None
            for axis in range(3):
                offset = tall[part, axis : axis + 1] - coords[axis : axis + 1, :]
                term = offset * offset
                square = term if square is None else square + term
            scaled = jnp.sqrt(square)
            tiles[t, part, :] = ((1.0 + scaled) * jnp.exp(-scaled)).astype(BF16)

    lane = lax.broadcasted_iota(jnp.int32, (rows, width), 1)
    halves = 2 ** (total - cross - 1)
    half = span // halves
    lane128 = lax.broadcasted_iota(jnp.int32, (rows, 128), 1)

    iterate = jnp.zeros_like(right)
    remain = right
    direction = right
    norm_now = None
    for it in range(ITERS):
        near = jnp.concatenate(
            [dot(low16[:, t * LEAF : (t + 1) * LEAF], tiles[t]) for t in range(count)], axis=1
        )
        local = [
            dot(low16[:, h * half : (h + 1) * half], basis_ref[upper:, h * half : (h + 1) * half], NT)
            for h in range(halves)
        ]
        spread = []
        for h in range(halves):
            cuts = []
            for depth in range(total - cross):
                size = halves // 2**depth
                first = h // size * size
                whole = local[first]
                for other in range(first + 1, first + size):
                    whole = whole + local[other]
                cuts.append(whole[:, depth * K : (depth + 1) * K])
            node = jnp.concatenate(cuts, axis=1).astype(BF16)
            spread.append(dot(node, basis_ref[upper:, h * half : (h + 1) * half]))
        result = near + NOISE * direction + jnp.concatenate(spread, axis=1)
        mine = jnp.sum(direction * result, axis=1, keepdims=True)
        more = it + 1 < ITERS
        whole_first = fused and it == 0
        if whole_first:
            pass
        elif fused:
            parts = [mine, jnp.sum(remain * remain, axis=1, keepdims=True)]
            message = jnp.zeros((rows, width), F32)
            if more:
                unit = result * shrink
                wide = unit.astype(BF16).astype(F32)
                both = jnp.concatenate([wide, unit - wide], axis=0).astype(BF16)
                seen = dot(both, basis_ref[:upper, :], NT)
                seen = seen[:rows] + seen[rows:]
                message = jnp.concatenate([seen, jnp.zeros((rows, width - upper), F32)], axis=1)
                parts += [
                    jnp.sum(unit * unit, axis=1, keepdims=True),
                    jnp.sum(remain * result, axis=1, keepdims=True),
                ]
            for i, part in enumerate(parts):
                message = jnp.where(lane == upper + i, part, message)
            scalars[it, 0] = message
        elif it == 0:
            first_norm = jnp.sum(remain * remain, axis=1, keepdims=True)
            scalars[it, 0] = jnp.where(lane128 < 64, mine, first_norm)
        else:
            scalars[it, 0] = jnp.broadcast_to(mine, (rows, 128))
        if not whole_first:
            broadcast(scalars, it, ITERS + it)
        if fused and it == 1:
            arrived_gram = gram.at[core, pl.ds(1, n - 1)]
            pltpu.make_async_copy(arrived_gram, arrived_gram, recv_sem.at[gram_sem]).wait()
            swap(swap_sem).start()

        arrived(sums, it, it)
        levels = tree_levels([sums[it, j] for j in range(n)])
        node = jnp.zeros((rows, width), F32)
        cover = jnp.zeros((rows, width), F32)
        for depth in range(cross):
            here = (lane >= depth * K) & (lane < (depth + 1) * K)
            nodes = levels[cross - depth]
            node = jnp.where(here, nodes[0][:rows], node)
            terms = [s[:rows].astype(BF16).astype(F32) * (s[:rows] + s[rows:]) for s in nodes]
            cover = jnp.where(here, tree_levels(terms)[-1][0], cover)
        result = result + dot(node[:, :upper].astype(BF16), basis_ref[:upper, :])
        cover = jnp.sum(cover, axis=1, keepdims=True)
        if whole_first:
            size = jnp.maximum(jnp.max(jnp.abs(result), axis=1, keepdims=True), 1e-30)
            shrink = 1.0 / size
            unit = result * shrink
            message = jnp.zeros((rows, width), F32)
            for i, part in enumerate(
                [
                    jnp.sum(direction * result, axis=1, keepdims=True),
                    jnp.sum(remain * remain, axis=1, keepdims=True),
                    jnp.sum(unit * unit, axis=1, keepdims=True),
                    size,
                ]
            ):
                message = jnp.where(lane == upper + i, part, message)
            scalars[it, 0] = message
            broadcast(scalars, it, ITERS + it)
            send_gram()

        if fused:
            if more:
                chains, turned = [], []
                for p in range(n // 2):
                    chain = jnp.zeros((rows, width), F32)
                    full = jnp.zeros((rows, width), F32)
                    for depth in range(cross):
                        here = (lane >= depth * K) & (lane < (depth + 1) * K)
                        at = levels[cross - depth][p // 2 ** (cross - 1 - depth)]
                        chain = jnp.where(here, at[:rows].astype(BF16).astype(F32), chain)
                        if p % 2 ** (cross - 1 - depth) == 0:
                            full = jnp.where(here, at[:rows] + at[rows:], full)
                    chains.append(chain)
                    turned.append(full)
                if it > 0:
                    moved = [now - ratio * old for now, old in zip(turned, turned_old)]
                    terms = [chain * there for chain, there in zip(chains, moved)]
                    remain_cover = jnp.sum(tree_levels(terms)[-1][0], axis=1, keepdims=True)
                turned_old = turned
                if it == 1:
                    swap(swap_sem).wait_recv()
                    form_top = build_forms()
                if it > 0:
                    terms = []
                    for p in range(n // 2):
                        chain16 = chains[p][:, :upper].astype(BF16)
                        image = dot(chain16, forms[p, 0]) + (
                            dot(chain16, forms[p, 1]) + dot(chain16, forms[p, 2])
                        )
                        terms.append(image * chains[p][:, :upper])
                    form = jnp.sum(tree_levels(terms)[-1][0], axis=1, keepdims=True)

            arrived(scalars, it, ITERS + it)
            got = [scalars[it, j] for j in range(n)]
            gathered = tree_levels(got)[-1][0]
            curve = gathered[:, upper : upper + 1]
            if it > 0:
                curve = curve + cover
            norm_now = gathered[:, upper + 1 : upper + 2]
            alpha = norm_now / curve
            if more and it == 0:
                sizes = [row[:, upper + 3 : upper + 4] for row in got]
                terms = []
                for j in range(n):
                    reach = alpha * sizes[j]
                    terms.append(reach * (reach * got[j][:, upper + 2 : upper + 3]))
                spent = tree_levels(terms)[-1][0]
                norm_next = (norm_now - 2.0 * (alpha * curve)) + spent
                ratio = norm_next / norm_now
            elif more:
                terms = []
                for j in range(n):
                    reach = alpha * sizes[j]
                    factors = jnp.where(
                        lane < upper,
                        (2.0 * alpha) * chains[j // 2],
                        jnp.where(lane == upper + 2, reach, 0.0),
                    )
                    terms.append(reach * (factors * got[j]))
                spent = jnp.sum(tree_levels(terms)[-1][0], axis=1, keepdims=True)
                crossed = alpha * (gathered[:, upper + 3 : upper + 4] + remain_cover)
                norm_next = (norm_now - 2.0 * crossed) + (spent + (alpha * form_top) * (alpha * form))
                ratio = norm_next / norm_now
            iterate = iterate + alpha * direction
            remain = remain - alpha * result
            if more:
                direction = remain + ratio * direction
                low16 = project_and_send(direction, it + 1)
            continue

        arrived(scalars, it, ITERS + it)
        gathered = tree_levels([scalars[it, j] for j in range(n)])[-1][0]
        curve = gathered[:, :1] + cover
        if it == 0:
            norm_now = gathered[:, 64:65]
        alpha = norm_now / curve
        remain = remain - alpha * result
        if it + 1 < ITERS:
            at = ITERS + it
            scalars[at, 0] = jnp.broadcast_to(
                jnp.sum(remain * remain, axis=1, keepdims=True), (rows, 128)
            )
            broadcast(scalars, at, ITERS + at)
            iterate = iterate + alpha * direction
            arrived(scalars, at, ITERS + at)
            norm_next = tree_levels([scalars[at, j] for j in range(n)])[-1][0][:, :1]
            direction = remain + norm_next / norm_now * direction
            norm_now = norm_next
            low16 = project_and_send(direction, it + 1)
        else:
            iterate = iterate + alpha * direction

    for t in range(count):
        cols = slice(t * LEAF, (t + 1) * LEAF)
        both = jnp.concatenate([iterate[:, cols], remain[:, cols]], axis=0)
        placed = join3(dot(split3(both), picks[t], NT))
        solution_ref[:, cols] = placed[:rows]
        residual_ref[:, cols] = placed[rows:]
    for it in range(ITERS):
        left(sums, it, it)
    for at in range(ITERS if fused else 2 * ITERS - 1):
        left(scalars, at, ITERS + at)
    if fused:
        sent = gram.at[core, pl.ds(1, n - 1)]
        pltpu.make_async_copy(sent, sent, send_sem.at[gram_sem]).wait()
        swap(swap_sem).wait_send()


def body(rhs, points, basis, tree_order, lengthscale):
    rows, span = rhs.shape
    n = lax.axis_size("leaf")
    cross = n.bit_length() - 1
    total = basis.shape[0] // K
    fused = n == 8
    width = -(-(cross * K + 64) // 128) * 128
    vmem = pl.BlockSpec(memory_space=pltpu.VMEM)
    hbm = pl.BlockSpec(memory_space=pltpu.MemorySpace.HBM)
    rounds = 3 * ITERS - 1

    def kernel(*refs):
        if not fused:
            refs = refs[:11] + (None, None) + refs[11:]
        cg_kernel(n, cross, total, *refs)

    return pl.pallas_call(
        kernel,
        out_shape=[jax.ShapeDtypeStruct((rows, span), F32)] * 2,
        in_specs=[hbm, hbm, hbm, hbm, pl.BlockSpec(memory_space=pltpu.SMEM)],
        out_specs=[vmem, vmem],
        scratch_shapes=[shape for shape in [
            pltpu.VMEM((span // LEAF, LEAF, LEAF), BF16),
            pltpu.VMEM((span // LEAF, LEAF, LEAF), BF16),
            pltpu.VMEM((ITERS, n, 2 * rows, width), F32),
            pltpu.VMEM((ITERS, n, rows, width) if fused else (2 * ITERS - 1, n, rows, 128), F32),
            pltpu.VMEM((2, n, K * 3 // 2, 128), F32) if fused else None,
            pltpu.VMEM((n // 2, 3, cross * K, cross * K), BF16) if fused else None,
            pltpu.VMEM((rows, span), F32),
            pltpu.VMEM((3, span), F32),
            pltpu.VMEM(basis.shape, BF16),
            pltpu.VMEM((1, span), jnp.int32),
            pltpu.SemaphoreType.DMA((rounds,)),
            pltpu.SemaphoreType.DMA((rounds,)),
            pltpu.SemaphoreType.DMA((4,)),
        ] if shape is not None],
        compiler_params=pltpu.CompilerParams(
            collective_id=0, has_side_effects=True, vmem_limit_bytes=63 * 2**20
        ),
        name="cg",
    )(rhs, points, basis, tree_order.reshape(1, span), lengthscale)


def solution(mesh):
    in_specs = (
        P("probe", ("groups", "leaf")),
        P(None, ("groups", "leaf")),
        P(None, ("groups", "leaf")),
        P(("groups", "leaf")),
        P("groups"),
    )
    out_specs = (P("probe", ("groups", "leaf")), P("probe", ("groups", "leaf")))
    return jax.shard_map(body, mesh=mesh, in_specs=in_specs, out_specs=out_specs, check_vma=False)
```

```python
import functools

import jax
import jax.numpy as jnp
from jax import lax
from jax.experimental import pallas as pl
from jax.experimental.pallas import tpu as pltpu
from jax.sharding import PartitionSpec as P

LEAF = 512
K = 64
ITERS = 4
CHUNK = 128

NOISE = 0.5
ROOT_THREE = 1.7320508
F32 = jnp.float32
BF16 = jnp.bfloat16
NN = (((1,), (0,)), ((), ()))
NT = (((1,), (1,)), ((), ()))


def dot(a, b, dims=NN):
    return lax.dot_general(a, b, dims, preferred_element_type=F32)


def split3(x):
    hi = x.astype(BF16)
    rest = x - hi.astype(F32)
    mid = rest.astype(BF16)
    low = (rest - mid.astype(F32)).astype(BF16)
    return jnp.concatenate([hi.astype(F32), mid.astype(F32), low.astype(F32)], axis=0).astype(BF16)


def join3(y):
    rows = y.shape[0] // 3
    return y[:rows] + (y[rows : 2 * rows] + y[2 * rows :])


def tree_levels(leaves):
    levels = [leaves]
    while len(levels[-1]) > 1:
        last = levels[-1]
        levels.append([last[2 * i] + last[2 * i + 1] for i in range(len(last) // 2)])
    return levels


def cg_kernel(
    n,
    cross,
    total,
    rhs_hbm,
    points_hbm,
    basis_hbm,
    order_hbm,
    scale_ref,
    solution_ref,
    residual_ref,
    tiles,
    picks,
    sums,
    scalars,
    gram,
    gram_own,
    gram_inbox,
    forms,
    rhs_ref,
    points_ref,
    basis_ref,
    order_ref,
    send_sem,
    recv_sem,
    load_sem,
):
    me = lax.axis_index("leaf")
    core = lax.axis_index("probe")
    fused = gram is not None
    rows, span = rhs_ref.shape
    count = span // LEAF
    upper = cross * K
    width = sums.shape[-1]

    def partner(slot):
        other = me
        for b in range(cross):
            bit = (slot // 2**b) % 2
            mine = (me // 2**b) % 2
            other = other + bit * (1 - 2 * mine) * 2**b
        return other

    def each_partner(act):
        if n <= 8:
            for slot in range(1, n):
                act(slot)
        else:
            def step(slot, carry):
                act(slot)
                return carry
            lax.fori_loop(1, n, step, 0)

    def broadcast(buffer, at, sem):
        def act(slot):
            pltpu.make_async_remote_copy(
                src_ref=buffer.at[at, 0],
                dst_ref=buffer.at[at, slot],
                send_sem=send_sem.at[sem],
                recv_sem=recv_sem.at[sem],
                device_id={"leaf": partner(slot)},
                device_id_type=pl.DeviceIdType.MESH,
            ).start()
        each_partner(act)

    def arrived(buffer, at, sem):
        landed = buffer.at[at, pl.ds(1, n - 1)]
        pltpu.make_async_copy(landed, landed, recv_sem.at[sem]).wait()

    def left(buffer, at, sem):
        landed = buffer.at[at, pl.ds(1, n - 1)]
        pltpu.make_async_copy(landed, landed, send_sem.at[sem]).wait()

    sources = (order_hbm, rhs_hbm, basis_hbm, points_hbm)
    targets = (order_ref, rhs_ref, basis_ref, points_ref)
    loads = [
        pltpu.make_async_copy(source, target, load_sem.at[i])
        for i, (source, target) in enumerate(zip(sources, targets))
    ]
    for load in loads:
        load.start()

    barrier = pltpu.get_barrier_semaphore()

    def greet(slot):
        pl.semaphore_signal(
            barrier, inc=1, device_id={"leaf": partner(slot)}, device_id_type=pl.DeviceIdType.MESH
        )

    each_partner(greet)
    if fused:
        pl.semaphore_signal(
            barrier, inc=1, device_id={"probe": 1 - core}, device_id_type=pl.DeviceIdType.MESH
        )

    loads[0].wait()
    loads[1].wait()
    row_id = lax.broadcasted_iota(jnp.int32, (LEAF, LEAF), 0)
    right_parts = []
    for t in range(count):
        cols = slice(t * LEAF, (t + 1) * LEAF)
        wanted = order_ref[:, cols] % LEAF
        picks[t] = jnp.where(row_id == wanted, 1.0, 0.0).astype(BF16)
        right_parts.append(join3(dot(split3(rhs_ref[:, cols]), picks[t])))
    right = jnp.concatenate(right_parts, axis=1)

    def project_and_send(direction, it):
        low16 = direction.astype(BF16)
        wide = low16.astype(F32)
        both = jnp.concatenate([wide, direction - wide], axis=0).astype(BF16)
        sums[it, 0, :, :upper] = dot(both, basis_ref[:upper, :], NT)
        if it == 0:
            pl.semaphore_wait(barrier, n if fused else n - 1)
        broadcast(sums, it, it)
        return low16

    loads[2].wait()
    low16 = project_and_send(right, 0)

    side = me % 2

    def gram_copy(step, source, target, device):
        return pltpu.make_async_remote_copy(
            src_ref=source,
            dst_ref=target,
            send_sem=send_sem.at[2 * ITERS + step],
            recv_sem=recv_sem.at[2 * ITERS + step],
            device_id=device,
            device_id_type=pl.DeviceIdType.MESH,
        )

    def gram_first():
        return gram_copy(0, gram_own.at[core, 1 - side], gram_inbox, {"leaf": partner(1)})

    def gram_second(p):
        return gram_copy(
            1, gram.at[core, side, 0], gram.at[core, side, p], {"leaf": partner(2 * p)}
        )

    def gram_third():
        return gram_copy(2, gram.at[core, side], gram.at[core, side], {"leaf": partner(1)})

    def gram_fourth():
        return gram_copy(3, gram.at[core], gram.at[core], {"probe": 1 - core})

    def gram_others():
        return gram.at[core, side, pl.ds(1, n // 2 - 1)]

    if fused:
        square = dot(basis_ref[:upper, :], basis_ref[:upper, :], NT)
        first = square[:K, :]
        second = jnp.concatenate([square[K : 2 * K, K:], square[2 * K :, 2 * K :]], axis=1)
        for h, block in enumerate((first, second)):
            tail = jnp.concatenate([block[: K // 2, 128:], block[K // 2 :, 128:]], axis=1)
            packed = jnp.concatenate([block[:, :128], tail], axis=0)
            gram_own[h, 0] = packed[:48]
            gram_own[h, 1] = packed[48:]
        gram_first().start()

    def build_forms():
        pairs = []
        for p in range(n // 2):
            rows_of = []
            for h in range(2):
                packed = jnp.concatenate([gram[h, 0, p], gram[h, 1, p]], axis=0)
                tail = jnp.concatenate([packed[K:, :K], packed[K:, K:]], axis=0)
                rows_of.append(jnp.concatenate([packed[:K], tail], axis=1))
            pairs.append(rows_of)
        top = functools.reduce(jnp.maximum, [jnp.abs(block) for blocks in pairs for block in blocks])
        top = jnp.max(jnp.max(top, axis=1, keepdims=True), axis=0, keepdims=True)
        top = jnp.maximum(top, 1e-30)
        turn = 1.0 / top
        lane_k = lax.broadcasted_iota(jnp.int32, (K, upper), 1)
        for p, (a, b) in enumerate(pairs):
            none = jnp.zeros((K, K), F32)
            grid = [
                jnp.where(lane_k < K, a, 2.0 * a),
                jnp.concatenate([none, b[:, :K], 2.0 * b[:, K : 2 * K]], axis=1),
                jnp.concatenate([none, none, b[:, 2 * K :]], axis=1),
            ]
            whole = jnp.concatenate(grid, axis=0) * turn
            hi = whole.astype(BF16)
            rest = whole - hi.astype(F32)
            mid = rest.astype(BF16)
            low = (rest - mid.astype(F32)).astype(BF16)
            forms[p, 0] = hi
            forms[p, 1] = mid
            forms[p, 2] = low
        return top

    loads[3].wait()
    factor = ROOT_THREE / scale_ref[0]
    for t in range(count):
        cols = slice(t * LEAF, (t + 1) * LEAF)
        coords = points_ref[:, cols] * factor
        tall = jnp.transpose(
            jnp.concatenate([coords, jnp.zeros((5, LEAF), F32)], axis=0)
        )
        for c in range(LEAF // CHUNK):
            part = slice(c * CHUNK, (c + 1) * CHUNK)
            square = None
            for axis in range(3):
                offset = tall[part, axis : axis + 1] - coords[axis : axis + 1, :]
                term = offset * offset
                square = term if square is None else square + term
            scaled = jnp.sqrt(square)
            tiles[t, part, :] = ((1.0 + scaled) * jnp.exp(-scaled)).astype(BF16)

    if fused:
        gram_first().wait_recv()
        gram[core, side, 0] = gram_own[core, side] + gram_inbox[...]
        for p in range(1, n // 2):
            gram_second(p).start()

    lane = lax.broadcasted_iota(jnp.int32, (rows, width), 1)
    halves = 2 ** (total - cross - 1)
    half = span // halves
    lane128 = lax.broadcasted_iota(jnp.int32, (rows, 128), 1)

    iterate = jnp.zeros_like(right)
    remain = right
    direction = right
    norm_now = None
    for it in range(ITERS):
        if fused and it == 1:
            gram_third().wait_recv()
            gram_fourth().start()
        near = jnp.concatenate(
            [dot(low16[:, t * LEAF : (t + 1) * LEAF], tiles[t]) for t in range(count)], axis=1
        )
        local = [
            dot(low16[:, h * half : (h + 1) * half], basis_ref[upper:, h * half : (h + 1) * half], NT)
            for h in range(halves)
        ]
        spread = []
        for h in range(halves):
            cuts = []
            for depth in range(total - cross):
                size = halves // 2**depth
                first = h // size * size
                whole = local[first]
                for other in range(first + 1, first + size):
                    whole = whole + local[other]
                cuts.append(whole[:, depth * K : (depth + 1) * K])
            node = jnp.concatenate(cuts, axis=1).astype(BF16)
            spread.append(dot(node, basis_ref[upper:, h * half : (h + 1) * half]))
        result = near + NOISE * direction + jnp.concatenate(spread, axis=1)
        mine = jnp.sum(direction * result, axis=1, keepdims=True)
        more = it + 1 < ITERS
        whole_first = fused and it == 0
        if whole_first:
            pass
        elif fused:
            parts = [mine, jnp.sum(remain * remain, axis=1, keepdims=True)]
            message = jnp.zeros((rows, width), F32)
            if more:
                unit = result * shrink
                wide = unit.astype(BF16).astype(F32)
                both = jnp.concatenate([wide, unit - wide], axis=0).astype(BF16)
                seen = dot(both, basis_ref[:upper, :], NT)
                seen = seen[:rows] + seen[rows:]
                message = jnp.concatenate([seen, jnp.zeros((rows, width - upper), F32)], axis=1)
                parts += [
                    jnp.sum(unit * unit, axis=1, keepdims=True),
                    jnp.sum(remain * result, axis=1, keepdims=True),
                ]
            for i, part in enumerate(parts):
                message = jnp.where(lane == upper + i, part, message)
            scalars[it, 0] = message
        elif it == 0:
            first_norm = jnp.sum(remain * remain, axis=1, keepdims=True)
            scalars[it, 0] = jnp.where(lane128 < 64, mine, first_norm)
        else:
            scalars[it, 0] = jnp.broadcast_to(mine, (rows, 128))
        if not whole_first:
            broadcast(scalars, it, ITERS + it)

        arrived(sums, it, it)
        levels = tree_levels([sums[it, j] for j in range(n)])
        node = jnp.zeros((rows, width), F32)
        cover = jnp.zeros((rows, width), F32)
        for depth in range(cross):
            here = (lane >= depth * K) & (lane < (depth + 1) * K)
            nodes = levels[cross - depth]
            node = jnp.where(here, nodes[0][:rows], node)
            terms = [s[:rows].astype(BF16).astype(F32) * (s[:rows] + s[rows:]) for s in nodes]
            cover = jnp.where(here, tree_levels(terms)[-1][0], cover)
        result = result + dot(node[:, :upper].astype(BF16), basis_ref[:upper, :])
        cover = jnp.sum(cover, axis=1, keepdims=True)
        if whole_first:
            size = jnp.maximum(jnp.max(jnp.abs(result), axis=1, keepdims=True), 1e-30)
            shrink = 1.0 / size
            unit = result * shrink
            message = jnp.zeros((rows, width), F32)
            for i, part in enumerate(
                [
                    jnp.sum(direction * result, axis=1, keepdims=True),
                    jnp.sum(remain * remain, axis=1, keepdims=True),
                    jnp.sum(unit * unit, axis=1, keepdims=True),
                    size,
                ]
            ):
                message = jnp.where(lane == upper + i, part, message)
            scalars[it, 0] = message
            broadcast(scalars, it, ITERS + it)
            others = gram_others()
            pltpu.make_async_copy(others, others, recv_sem.at[2 * ITERS + 1]).wait()
            gram_third().start()

        if fused:
            if more:
                chains, turned = [], []
                for p in range(n // 2):
                    chain = jnp.zeros((rows, width), F32)
                    full = jnp.zeros((rows, width), F32)
                    for depth in range(cross):
                        here = (lane >= depth * K) & (lane < (depth + 1) * K)
                        at = levels[cross - depth][p // 2 ** (cross - 1 - depth)]
                        chain = jnp.where(here, at[:rows].astype(BF16).astype(F32), chain)
                        if p % 2 ** (cross - 1 - depth) == 0:
                            full = jnp.where(here, at[:rows] + at[rows:], full)
                    chains.append(chain)
                    turned.append(full)
                if it > 0:
                    moved = [now - ratio * old for now, old in zip(turned, turned_old)]
                    terms = [chain * there for chain, there in zip(chains, moved)]
                    remain_cover = jnp.sum(tree_levels(terms)[-1][0], axis=1, keepdims=True)
                turned_old = turned
                if it == 1:
                    gram_fourth().wait_recv()
                    form_top = build_forms()
                if it > 0:
                    terms = []
                    for p in range(n // 2):
                        chain16 = chains[p][:, :upper].astype(BF16)
                        image = dot(chain16, forms[p, 0]) + (
                            dot(chain16, forms[p, 1]) + dot(chain16, forms[p, 2])
                        )
                        terms.append(image * chains[p][:, :upper])
                    form = jnp.sum(tree_levels(terms)[-1][0], axis=1, keepdims=True)

            arrived(scalars, it, ITERS + it)
            got = [scalars[it, j] for j in range(n)]
            gathered = tree_levels(got)[-1][0]
            curve = gathered[:, upper : upper + 1]
            if it > 0:
                curve = curve + cover
            norm_now = gathered[:, upper + 1 : upper + 2]
            alpha = norm_now / curve
            if more and it == 0:
                sizes = [row[:, upper + 3 : upper + 4] for row in got]
                terms = []
                for j in range(n):
                    reach = alpha * sizes[j]
                    terms.append(reach * (reach * got[j][:, upper + 2 : upper + 3]))
                spent = tree_levels(terms)[-1][0]
                norm_next = (norm_now - 2.0 * (alpha * curve)) + spent
                ratio = norm_next / norm_now
            elif more:
                terms = []
                for j in range(n):
                    reach = alpha * sizes[j]
                    factors = jnp.where(
                        lane < upper,
                        (2.0 * alpha) * chains[j // 2],
                        jnp.where(lane == upper + 2, reach, 0.0),
                    )
                    terms.append(reach * (factors * got[j]))
                spent = jnp.sum(tree_levels(terms)[-1][0], axis=1, keepdims=True)
                crossed = alpha * (gathered[:, upper + 3 : upper + 4] + remain_cover)
                norm_next = (norm_now - 2.0 * crossed) + (spent + (alpha * form_top) * (alpha * form))
                ratio = norm_next / norm_now
            iterate = iterate + alpha * direction
            remain = remain - alpha * result
            if more:
                direction = remain + ratio * direction
                low16 = project_and_send(direction, it + 1)
            continue

        arrived(scalars, it, ITERS + it)
        gathered = tree_levels([scalars[it, j] for j in range(n)])[-1][0]
        curve = gathered[:, :1] + cover
        if it == 0:
            norm_now = gathered[:, 64:65]
        alpha = norm_now / curve
        remain = remain - alpha * result
        if it + 1 < ITERS:
            at = ITERS + it
            scalars[at, 0] = jnp.broadcast_to(
                jnp.sum(remain * remain, axis=1, keepdims=True), (rows, 128)
            )
            broadcast(scalars, at, ITERS + at)
            iterate = iterate + alpha * direction
            arrived(scalars, at, ITERS + at)
            norm_next = tree_levels([scalars[at, j] for j in range(n)])[-1][0][:, :1]
            direction = remain + norm_next / norm_now * direction
            norm_now = norm_next
            low16 = project_and_send(direction, it + 1)
        else:
            iterate = iterate + alpha * direction

    for t in range(count):
        cols = slice(t * LEAF, (t + 1) * LEAF)
        both = jnp.concatenate([iterate[:, cols], remain[:, cols]], axis=0)
        placed = join3(dot(split3(both), picks[t], NT))
        solution_ref[:, cols] = placed[:rows]
        residual_ref[:, cols] = placed[rows:]
    for it in range(ITERS):
        left(sums, it, it)
    for at in range(ITERS if fused else 2 * ITERS - 1):
        left(scalars, at, ITERS + at)
    if fused:
        gram_first().wait_send()
        others = gram_others()
        pltpu.make_async_copy(others, others, send_sem.at[2 * ITERS + 1]).wait()
        gram_third().wait_send()
        gram_fourth().wait_send()


def body(rhs, points, basis, tree_order, lengthscale):
    rows, span = rhs.shape
    n = lax.axis_size("leaf")
    cross = n.bit_length() - 1
    total = basis.shape[0] // K
    fused = n == 8
    width = -(-(cross * K + 64) // 128) * 128
    vmem = pl.BlockSpec(memory_space=pltpu.VMEM)
    hbm = pl.BlockSpec(memory_space=pltpu.MemorySpace.HBM)
    rounds = 3 * ITERS

    def kernel(*refs):
        if not fused:
            refs = refs[:11] + (None,) * 4 + refs[11:]
        cg_kernel(n, cross, total, *refs)

    return pl.pallas_call(
        kernel,
        out_shape=[jax.ShapeDtypeStruct((rows, span), F32)] * 2,
        in_specs=[hbm, hbm, hbm, hbm, pl.BlockSpec(memory_space=pltpu.SMEM)],
        out_specs=[vmem, vmem],
        scratch_shapes=[shape for shape in [
            pltpu.VMEM((span // LEAF, LEAF, LEAF), BF16),
            pltpu.VMEM((span // LEAF, LEAF, LEAF), BF16),
            pltpu.VMEM((ITERS, n, 2 * rows, width), F32),
            pltpu.VMEM((ITERS, n, rows, width) if fused else (2 * ITERS - 1, n, rows, 128), F32),
            pltpu.VMEM((2, 2, n // 2, K * 3 // 4, 128), F32) if fused else None,
            pltpu.VMEM((2, 2, K * 3 // 4, 128), F32) if fused else None,
            pltpu.VMEM((K * 3 // 4, 128), F32) if fused else None,
            pltpu.VMEM((n // 2, 3, cross * K, cross * K), BF16) if fused else None,
            pltpu.VMEM((rows, span), F32),
            pltpu.VMEM((3, span), F32),
            pltpu.VMEM(basis.shape, BF16),
            pltpu.VMEM((1, span), jnp.int32),
            pltpu.SemaphoreType.DMA((rounds,)),
            pltpu.SemaphoreType.DMA((rounds,)),
            pltpu.SemaphoreType.DMA((4,)),
        ] if shape is not None],
        compiler_params=pltpu.CompilerParams(
            collective_id=0, has_side_effects=True, vmem_limit_bytes=63 * 2**20
        ),
        name="cg",
    )(rhs, points, basis, tree_order.reshape(1, span), lengthscale)


def solution(mesh):
    in_specs = (
        P("probe", ("groups", "leaf")),
        P(None, ("groups", "leaf")),
        P(None, ("groups", "leaf")),
        P(("groups", "leaf")),
        P("groups"),
    )
    out_specs = (P("probe", ("groups", "leaf")), P("probe", ("groups", "leaf")))
    return jax.shard_map(body, mesh=mesh, in_specs=in_specs, out_specs=out_specs, check_vma=False)
```

```python
import functools

import jax
import jax.numpy as jnp
from jax import lax
from jax.experimental import pallas as pl
from jax.experimental.pallas import tpu as pltpu
from jax.sharding import PartitionSpec as P

LEAF = 512
K = 64
ITERS = 4
CHUNK = 128

NOISE = 0.5
ROOT_THREE = 1.7320508
F32 = jnp.float32
BF16 = jnp.bfloat16
NN = (((1,), (0,)), ((), ()))
NT = (((1,), (1,)), ((), ()))


def dot(a, b, dims=NN):
    return lax.dot_general(a, b, dims, preferred_element_type=F32)


def split3(x):
    hi = x.astype(BF16)
    rest = x - hi.astype(F32)
    mid = rest.astype(BF16)
    low = (rest - mid.astype(F32)).astype(BF16)
    return jnp.concatenate([hi.astype(F32), mid.astype(F32), low.astype(F32)], axis=0).astype(BF16)


def join3(y):
    rows = y.shape[0] // 3
    return y[:rows] + (y[rows : 2 * rows] + y[2 * rows :])


def tree_levels(leaves):
    levels = [leaves]
    while len(levels[-1]) > 1:
        last = levels[-1]
        levels.append([last[2 * i] + last[2 * i + 1] for i in range(len(last) // 2)])
    return levels


def cg_kernel(
    n,
    cross,
    total,
    rhs_hbm,
    points_hbm,
    basis_hbm,
    order_hbm,
    scale_ref,
    both_ref,
    tiles,
    picks,
    sums,
    scalars,
    gram,
    gram_own,
    gram_inbox,
    forms,
    rhs_ref,
    points_ref,
    basis_ref,
    order_ref,
    send_sem,
    recv_sem,
    load_sem,
):
    me = lax.axis_index("leaf")
    core = lax.axis_index("probe")
    fused = gram is not None
    rows, span = rhs_ref.shape
    count = span // LEAF
    upper = cross * K
    width = sums.shape[-1]

    def partner(slot):
        other = me
        for b in range(cross):
            bit = (slot // 2**b) % 2
            mine = (me // 2**b) % 2
            other = other + bit * (1 - 2 * mine) * 2**b
        return other

    known = [partner(slot) for slot in range(n)] if n <= 8 else None

    def to(slot):
        return known[slot] if known is not None else partner(slot)

    def each_partner(act):
        if n <= 8:
            for slot in ([6, 7, 4, 5, 2, 3, 1] if n == 8 else range(1, n)):
                act(slot)
        else:
            def step(slot, carry):
                act(slot)
                return carry
            lax.fori_loop(1, n, step, 0)

    def broadcast(buffer, at, sem):
        def act(slot):
            pltpu.make_async_remote_copy(
                src_ref=buffer.at[at, 0],
                dst_ref=buffer.at[at, slot],
                send_sem=send_sem.at[sem],
                recv_sem=recv_sem.at[sem],
                device_id={"leaf": to(slot)},
                device_id_type=pl.DeviceIdType.MESH,
            ).start()
        each_partner(act)

    def arrived(buffer, at, sem):
        landed = buffer.at[at, pl.ds(1, n - 1)]
        pltpu.make_async_copy(landed, landed, recv_sem.at[sem]).wait()

    def left(buffer, at, sem):
        landed = buffer.at[at, pl.ds(1, n - 1)]
        pltpu.make_async_copy(landed, landed, send_sem.at[sem]).wait()

    sources = (order_hbm, rhs_hbm, basis_hbm, points_hbm)
    targets = (order_ref, rhs_ref, basis_ref, points_ref)
    loads = [
        pltpu.make_async_copy(source, target, load_sem.at[i])
        for i, (source, target) in enumerate(zip(sources, targets))
    ]
    for load in loads:
        load.start()

    barrier = pltpu.get_barrier_semaphore()

    def greet(slot):
        pl.semaphore_signal(
            barrier, inc=1, device_id={"leaf": to(slot)}, device_id_type=pl.DeviceIdType.MESH
        )

    each_partner(greet)
    if fused:
        pl.semaphore_signal(
            barrier, inc=1, device_id={"probe": 1 - core}, device_id_type=pl.DeviceIdType.MESH
        )

    loads[0].wait()
    loads[1].wait()
    row_id = lax.broadcasted_iota(jnp.int32, (LEAF, LEAF), 0)
    right_parts = []
    for t in range(count):
        cols = slice(t * LEAF, (t + 1) * LEAF)
        wanted = order_ref[:, cols] % LEAF
        picks[t] = jnp.where(row_id == wanted, 1.0, 0.0).astype(BF16)
        right_parts.append(join3(dot(split3(rhs_ref[:, cols]), picks[t])))
    right = jnp.concatenate(right_parts, axis=1)

    def project_and_send(direction, it):
        low16 = direction.astype(BF16)
        wide = low16.astype(F32)
        both = jnp.concatenate([wide, direction - wide], axis=0).astype(BF16)
        sums[it, 0, :, :upper] = dot(both, basis_ref[:upper, :], NT)
        if it == 0:
            pl.semaphore_wait(barrier, n if fused else n - 1)
        broadcast(sums, it, it)
        return low16

    loads[2].wait()
    low16 = project_and_send(right, 0)

    side = me % 2

    def gram_copy(step, source, target, device):
        return pltpu.make_async_remote_copy(
            src_ref=source,
            dst_ref=target,
            send_sem=send_sem.at[2 * ITERS + step],
            recv_sem=recv_sem.at[2 * ITERS + step],
            device_id=device,
            device_id_type=pl.DeviceIdType.MESH,
        )

    def gram_first():
        return gram_copy(0, gram_own.at[core, 1 - side], gram_inbox, {"leaf": to(1)})

    def gram_second(p):
        return gram_copy(
            1, gram.at[core, side, 0], gram.at[core, side, p], {"leaf": to(2 * p)}
        )

    def gram_third():
        return gram_copy(2, gram.at[core, side], gram.at[core, side], {"leaf": to(1)})

    def gram_fourth():
        return gram_copy(3, gram.at[core], gram.at[core], {"probe": 1 - core})

    def gram_others():
        return gram.at[core, side, pl.ds(1, n // 2 - 1)]

    if fused:
        square = dot(basis_ref[:upper, :], basis_ref[:upper, :], NT)
        first = square[:K, :]
        second = jnp.concatenate([square[K : 2 * K, K:], square[2 * K :, 2 * K :]], axis=1)
        for h, block in enumerate((first, second)):
            tail = jnp.concatenate([block[: K // 2, 128:], block[K // 2 :, 128:]], axis=1)
            packed = jnp.concatenate([block[:, :128], tail], axis=0)
            gram_own[h, 0] = packed[:48]
            gram_own[h, 1] = packed[48:]
        gram_first().start()

    def build_forms():
        pairs = []
        for p in range(n // 2):
            rows_of = []
            for h in range(2):
                packed = jnp.concatenate([gram[h, 0, p], gram[h, 1, p]], axis=0)
                tail = jnp.concatenate([packed[K:, :K], packed[K:, K:]], axis=0)
                rows_of.append(jnp.concatenate([packed[:K], tail], axis=1))
            pairs.append(rows_of)
        top = functools.reduce(jnp.maximum, [jnp.abs(block) for blocks in pairs for block in blocks])
        top = jnp.max(jnp.max(top, axis=1, keepdims=True), axis=0, keepdims=True)
        top = jnp.maximum(top, 1e-30)
        turn = 1.0 / top
        lane_k = lax.broadcasted_iota(jnp.int32, (K, upper), 1)
        for p, (a, b) in enumerate(pairs):
            none = jnp.zeros((K, K), F32)
            grid = [
                jnp.where(lane_k < K, a, 2.0 * a),
                jnp.concatenate([none, b[:, :K], 2.0 * b[:, K : 2 * K]], axis=1),
                jnp.concatenate([none, none, b[:, 2 * K :]], axis=1),
            ]
            whole = jnp.concatenate(grid, axis=0) * turn
            hi = whole.astype(BF16)
            rest = whole - hi.astype(F32)
            mid = rest.astype(BF16)
            low = (rest - mid.astype(F32)).astype(BF16)
            forms[p, 0] = hi
            forms[p, 1] = mid
            forms[p, 2] = low
        return top

    loads[3].wait()
    factor = ROOT_THREE / scale_ref[0]
    for t in range(count):
        cols = slice(t * LEAF, (t + 1) * LEAF)
        coords = points_ref[:, cols] * factor
        tall = jnp.transpose(
            jnp.concatenate([coords, jnp.zeros((5, LEAF), F32)], axis=0)
        )
        for c in range(LEAF // CHUNK):
            part = slice(c * CHUNK, (c + 1) * CHUNK)
            square = None
            for axis in range(3):
                offset = tall[part, axis : axis + 1] - coords[axis : axis + 1, :]
                term = offset * offset
                square = term if square is None else square + term
            scaled = jnp.sqrt(square)
            tiles[t, part, :] = ((1.0 + scaled) * jnp.exp(-scaled)).astype(BF16)

    if fused:
        gram_first().wait_recv()
        gram[core, side, 0] = gram_own[core, side] + gram_inbox[...]
        for p in range(1, n // 2):
            gram_second(p).start()

    lane = lax.broadcasted_iota(jnp.int32, (rows, width), 1)
    halves = 2 ** (total - cross - 1)
    half = span // halves
    lane128 = lax.broadcasted_iota(jnp.int32, (rows, 128), 1)

    iterate = jnp.zeros_like(right)
    remain = right
    direction = right
    norm_now = None
    for it in range(ITERS):
        if fused and it == 1:
            gram_third().wait_recv()
            gram_fourth().start()
        near = jnp.concatenate(
            [dot(low16[:, t * LEAF : (t + 1) * LEAF], tiles[t]) for t in range(count)], axis=1
        )
        local = [
            dot(low16[:, h * half : (h + 1) * half], basis_ref[upper:, h * half : (h + 1) * half], NT)
            for h in range(halves)
        ]
        spread = []
        for h in range(halves):
            cuts = []
            for depth in range(total - cross):
                size = halves // 2**depth
                first = h // size * size
                whole = local[first]
                for other in range(first + 1, first + size):
                    whole = whole + local[other]
                cuts.append(whole[:, depth * K : (depth + 1) * K])
            node = jnp.concatenate(cuts, axis=1).astype(BF16)
            spread.append(dot(node, basis_ref[upper:, h * half : (h + 1) * half]))
        result = near + NOISE * direction + jnp.concatenate(spread, axis=1)
        mine = jnp.sum(direction * result, axis=1, keepdims=True)
        more = it + 1 < ITERS
        whole_first = fused and it == 0
        if whole_first:
            pass
        elif fused:
            parts = [mine, jnp.sum(remain * remain, axis=1, keepdims=True)]
            message = jnp.zeros((rows, width), F32)
            if more:
                unit = result * shrink
                wide = unit.astype(BF16).astype(F32)
                both = jnp.concatenate([wide, unit - wide], axis=0).astype(BF16)
                seen = dot(both, basis_ref[:upper, :], NT)
                seen = seen[:rows] + seen[rows:]
                message = jnp.concatenate([seen, jnp.zeros((rows, width - upper), F32)], axis=1)
                parts += [
                    jnp.sum(unit * unit, axis=1, keepdims=True),
                    jnp.sum(remain * result, axis=1, keepdims=True),
                ]
            for i, part in enumerate(parts):
                message = jnp.where(lane == upper + i, part, message)
            scalars[it, 0] = message
        elif it == 0:
            first_norm = jnp.sum(remain * remain, axis=1, keepdims=True)
            scalars[it, 0] = jnp.where(lane128 < 64, mine, first_norm)
        else:
            scalars[it, 0] = jnp.broadcast_to(mine, (rows, 128))
        if not whole_first:
            broadcast(scalars, it, ITERS + it)

        arrived(sums, it, it)
        levels = tree_levels([sums[it, j] for j in range(n)])
        node = jnp.zeros((rows, width), F32)
        cover = jnp.zeros((rows, width), F32)
        for depth in range(cross):
            here = (lane >= depth * K) & (lane < (depth + 1) * K)
            nodes = levels[cross - depth]
            node = jnp.where(here, nodes[0][:rows], node)
            terms = [s[:rows].astype(BF16).astype(F32) * (s[:rows] + s[rows:]) for s in nodes]
            cover = jnp.where(here, tree_levels(terms)[-1][0], cover)
        result = result + dot(node[:, :upper].astype(BF16), basis_ref[:upper, :])
        cover = jnp.sum(cover, axis=1, keepdims=True)
        if whole_first:
            size = jnp.maximum(jnp.max(jnp.abs(result), axis=1, keepdims=True), 1e-30)
            shrink = 1.0 / size
            unit = result * shrink
            message = jnp.zeros((rows, width), F32)
            for i, part in enumerate(
                [
                    jnp.sum(direction * result, axis=1, keepdims=True),
                    jnp.sum(remain * remain, axis=1, keepdims=True),
                    jnp.sum(unit * unit, axis=1, keepdims=True),
                    size,
                ]
            ):
                message = jnp.where(lane == upper + i, part, message)
            scalars[it, 0] = message
            broadcast(scalars, it, ITERS + it)
            others = gram_others()
            pltpu.make_async_copy(others, others, recv_sem.at[2 * ITERS + 1]).wait()
            gram_third().start()

        if fused:
            if more:
                chains, turned = [], []
                for p in range(n // 2):
                    chain = jnp.zeros((rows, width), F32)
                    full = jnp.zeros((rows, width), F32)
                    for depth in range(cross):
                        here = (lane >= depth * K) & (lane < (depth + 1) * K)
                        at = levels[cross - depth][p // 2 ** (cross - 1 - depth)]
                        chain = jnp.where(here, at[:rows].astype(BF16).astype(F32), chain)
                        if p % 2 ** (cross - 1 - depth) == 0:
                            full = jnp.where(here, at[:rows] + at[rows:], full)
                    chains.append(chain)
                    turned.append(full)
                if it > 0:
                    moved = [now - ratio * old for now, old in zip(turned, turned_old)]
                    terms = [chain * there for chain, there in zip(chains, moved)]
                    remain_cover = jnp.sum(tree_levels(terms)[-1][0], axis=1, keepdims=True)
                turned_old = turned
                if it == 1:
                    gram_fourth().wait_recv()
                    form_top = build_forms()
                if it > 0:
                    terms = []
                    for p in range(n // 2):
                        chain16 = chains[p][:, :upper].astype(BF16)
                        image = dot(chain16, forms[p, 0]) + (
                            dot(chain16, forms[p, 1]) + dot(chain16, forms[p, 2])
                        )
                        terms.append(image * chains[p][:, :upper])
                    form = jnp.sum(tree_levels(terms)[-1][0], axis=1, keepdims=True)

            arrived(scalars, it, ITERS + it)
            got = [scalars[it, j] for j in range(n)]
            gathered = tree_levels(got)[-1][0]
            curve = gathered[:, upper : upper + 1]
            if it > 0:
                curve = curve + cover
            norm_now = gathered[:, upper + 1 : upper + 2]
            alpha = norm_now / curve
            if more and it == 0:
                sizes = [row[:, upper + 3 : upper + 4] for row in got]
                terms = []
                for j in range(n):
                    reach = alpha * sizes[j]
                    terms.append(reach * (reach * got[j][:, upper + 2 : upper + 3]))
                spent = tree_levels(terms)[-1][0]
                norm_next = (norm_now - 2.0 * (alpha * curve)) + spent
                ratio = norm_next / norm_now
            elif more:
                terms = []
                for j in range(n):
                    reach = alpha * sizes[j]
                    factors = jnp.where(
                        lane < upper,
                        (2.0 * alpha) * chains[j // 2],
                        jnp.where(lane == upper + 2, reach, 0.0),
                    )
                    terms.append(reach * (factors * got[j]))
                spent = jnp.sum(tree_levels(terms)[-1][0], axis=1, keepdims=True)
                crossed = alpha * (gathered[:, upper + 3 : upper + 4] + remain_cover)
                norm_next = (norm_now - 2.0 * crossed) + (spent + (alpha * form_top) * (alpha * form))
                ratio = norm_next / norm_now
            iterate = iterate + alpha * direction
            remain = remain - alpha * result
            if more:
                direction = remain + ratio * direction
                low16 = project_and_send(direction, it + 1)
            continue

        arrived(scalars, it, ITERS + it)
        gathered = tree_levels([scalars[it, j] for j in range(n)])[-1][0]
        curve = gathered[:, :1] + cover
        if it == 0:
            norm_now = gathered[:, 64:65]
        alpha = norm_now / curve
        remain = remain - alpha * result
        if it + 1 < ITERS:
            at = ITERS + it
            scalars[at, 0] = jnp.broadcast_to(
                jnp.sum(remain * remain, axis=1, keepdims=True), (rows, 128)
            )
            broadcast(scalars, at, ITERS + at)
            iterate = iterate + alpha * direction
            arrived(scalars, at, ITERS + at)
            norm_next = tree_levels([scalars[at, j] for j in range(n)])[-1][0][:, :1]
            direction = remain + norm_next / norm_now * direction
            norm_now = norm_next
            low16 = project_and_send(direction, it + 1)
        else:
            iterate = iterate + alpha * direction

    for t in range(count):
        cols = slice(t * LEAF, (t + 1) * LEAF)
        both = jnp.concatenate([iterate[:, cols], remain[:, cols]], axis=0)
        placed = join3(dot(split3(both), picks[t], NT))
        both_ref[:, cols] = placed
    for it in range(ITERS):
        left(sums, it, it)
    for at in range(ITERS if fused else 2 * ITERS - 1):
        left(scalars, at, ITERS + at)
    if fused:
        gram_first().wait_send()
        others = gram_others()
        pltpu.make_async_copy(others, others, send_sem.at[2 * ITERS + 1]).wait()
        gram_third().wait_send()
        gram_fourth().wait_send()


def body(rhs, points, basis, tree_order, lengthscale):
    rows, span = rhs.shape
    n = lax.axis_size("leaf")
    cross = n.bit_length() - 1
    total = basis.shape[0] // K
    fused = n == 8
    width = -(-(cross * K + 64) // 128) * 128
    vmem = pl.BlockSpec(memory_space=pltpu.VMEM)
    hbm = pl.BlockSpec(memory_space=pltpu.MemorySpace.HBM)
    rounds = 3 * ITERS

    def kernel(*refs):
        if not fused:
            refs = refs[:10] + (None,) * 4 + refs[10:]
        cg_kernel(n, cross, total, *refs)

    both = pl.pallas_call(
        kernel,
        out_shape=pltpu.VMEM((2 * rows, span), F32),
        in_specs=[hbm, hbm, hbm, hbm, pl.BlockSpec(memory_space=pltpu.SMEM)],
        out_specs=vmem,
        scratch_shapes=[shape for shape in [
            pltpu.VMEM((span // LEAF, LEAF, LEAF), BF16),
            pltpu.VMEM((span // LEAF, LEAF, LEAF), BF16),
            pltpu.VMEM((ITERS, n, 2 * rows, width), F32),
            pltpu.VMEM((ITERS, n, rows, width) if fused else (2 * ITERS - 1, n, rows, 128), F32),
            pltpu.VMEM((2, 2, n // 2, K * 3 // 4, 128), F32) if fused else None,
            pltpu.VMEM((2, 2, K * 3 // 4, 128), F32) if fused else None,
            pltpu.VMEM((K * 3 // 4, 128), F32) if fused else None,
            pltpu.VMEM((n // 2, 3, cross * K, cross * K), BF16) if fused else None,
            pltpu.VMEM((rows, span), F32),
            pltpu.VMEM((3, span), F32),
            pltpu.VMEM(basis.shape, BF16),
            pltpu.VMEM((1, span), jnp.int32),
            pltpu.SemaphoreType.DMA((rounds,)),
            pltpu.SemaphoreType.DMA((rounds,)),
            pltpu.SemaphoreType.DMA((4,)),
        ] if shape is not None],
        compiler_params=pltpu.CompilerParams(
            collective_id=0, has_side_effects=True, vmem_limit_bytes=63 * 2**20
        ),
        name="cg",
    )(rhs, points, basis, tree_order.reshape(1, span), lengthscale)
    return both[:rows], both[rows:]


def solution(mesh):
    in_specs = (
        P("probe", ("groups", "leaf")),
        P(None, ("groups", "leaf")),
        P(None, ("groups", "leaf")),
        P(("groups", "leaf")),
        P("groups"),
    )
    out_specs = (P("probe", ("groups", "leaf")), P("probe", ("groups", "leaf")))
    return jax.shard_map(body, mesh=mesh, in_specs=in_specs, out_specs=out_specs, check_vma=False)
```

```python
import functools

import jax
import jax.numpy as jnp
from jax import lax
from jax.experimental import pallas as pl
from jax.experimental.pallas import tpu as pltpu
from jax.sharding import PartitionSpec as P

LEAF = 512
K = 64
ITERS = 4
CHUNK = 128

NOISE = 0.5
ROOT_THREE = 1.7320508
F32 = jnp.float32
BF16 = jnp.bfloat16
NN = (((1,), (0,)), ((), ()))
NT = (((1,), (1,)), ((), ()))


def dot(a, b, dims=NN):
    return lax.dot_general(a, b, dims, preferred_element_type=F32)


def split3(x):
    hi = x.astype(BF16)
    rest = x - hi.astype(F32)
    mid = rest.astype(BF16)
    low = (rest - mid.astype(F32)).astype(BF16)
    return jnp.concatenate([hi.astype(F32), mid.astype(F32), low.astype(F32)], axis=0).astype(BF16)


def join3(y):
    rows = y.shape[0] // 3
    return y[:rows] + (y[rows : 2 * rows] + y[2 * rows :])


def tree_levels(leaves):
    levels = [leaves]
    while len(levels[-1]) > 1:
        last = levels[-1]
        levels.append([last[2 * i] + last[2 * i + 1] for i in range(len(last) // 2)])
    return levels


def cg_kernel(
    n,
    cross,
    total,
    rhs_hbm,
    points_hbm,
    basis_hbm,
    order_hbm,
    scale_ref,
    both_ref,
    tiles,
    picks,
    sums,
    scalars,
    gram,
    gram_own,
    gram_inbox,
    forms,
    rhs_ref,
    points_ref,
    basis_ref,
    order_ref,
    send_sem,
    recv_sem,
    load_sem,
):
    me = lax.axis_index("leaf")
    core = lax.axis_index("probe")
    fused = gram is not None
    rows, span = rhs_ref.shape
    count = span // LEAF
    upper = cross * K
    width = sums.shape[-1]

    def partner(slot):
        other = me
        for b in range(cross):
            bit = (slot // 2**b) % 2
            mine = (me // 2**b) % 2
            other = other + bit * (1 - 2 * mine) * 2**b
        return other

    known = [partner(slot) for slot in range(n)] if n <= 8 else None

    def to(slot):
        return known[slot] if known is not None else partner(slot)

    def each_partner(act):
        if n <= 8:
            for slot in ([6, 7, 4, 5, 2, 3, 1] if n == 8 else range(1, n)):
                act(slot)
        else:
            def step(slot, carry):
                act(slot)
                return carry
            lax.fori_loop(1, n, step, 0)

    def broadcast(buffer, at, sem):
        def act(slot):
            pltpu.make_async_remote_copy(
                src_ref=buffer.at[at, 0],
                dst_ref=buffer.at[at, slot],
                send_sem=send_sem.at[sem],
                recv_sem=recv_sem.at[sem],
                device_id={"leaf": to(slot)},
                device_id_type=pl.DeviceIdType.MESH,
            ).start()
        each_partner(act)

    def arrived(buffer, at, sem):
        landed = buffer.at[at, pl.ds(1, n - 1)]
        pltpu.make_async_copy(landed, landed, recv_sem.at[sem]).wait()

    def left(buffer, at, sem):
        landed = buffer.at[at, pl.ds(1, n - 1)]
        pltpu.make_async_copy(landed, landed, send_sem.at[sem]).wait()

    sources = (order_hbm, rhs_hbm, basis_hbm, points_hbm)
    targets = (order_ref, rhs_ref, basis_ref, points_ref)
    loads = [
        pltpu.make_async_copy(source, target, load_sem.at[i])
        for i, (source, target) in enumerate(zip(sources, targets))
    ]
    for load in loads:
        load.start()

    barrier = pltpu.get_barrier_semaphore()

    def greet(slot):
        pl.semaphore_signal(
            barrier, inc=1, device_id={"leaf": to(slot)}, device_id_type=pl.DeviceIdType.MESH
        )

    each_partner(greet)
    if fused:
        pl.semaphore_signal(
            barrier, inc=1, device_id={"probe": 1 - core}, device_id_type=pl.DeviceIdType.MESH
        )

    loads[0].wait()
    loads[1].wait()
    row_id = lax.broadcasted_iota(jnp.int32, (LEAF, LEAF), 0)
    right_parts = []
    for t in range(count):
        cols = slice(t * LEAF, (t + 1) * LEAF)
        wanted = order_ref[:, cols] % LEAF
        picks[t] = jnp.where(row_id == wanted, 1.0, 0.0).astype(BF16)
        right_parts.append(join3(dot(split3(rhs_ref[:, cols]), picks[t])))
    right = jnp.concatenate(right_parts, axis=1)

    def project_and_send(direction, it):
        low16 = direction.astype(BF16)
        wide = low16.astype(F32)
        both = jnp.concatenate([wide, direction - wide], axis=0).astype(BF16)
        sums[it, 0, :, :upper] = dot(both, basis_ref[:upper, :], NT)
        if it == 0:
            pl.semaphore_wait(barrier, n if fused else n - 1)
        broadcast(sums, it, it)
        return low16

    loads[2].wait()
    low16 = project_and_send(right, 0)

    side = me % 2

    def gram_copy(step, source, target, device):
        return pltpu.make_async_remote_copy(
            src_ref=source,
            dst_ref=target,
            send_sem=send_sem.at[2 * ITERS + step],
            recv_sem=recv_sem.at[2 * ITERS + step],
            device_id=device,
            device_id_type=pl.DeviceIdType.MESH,
        )

    def gram_first():
        return gram_copy(0, gram_own.at[core, 1 - side], gram_inbox, {"leaf": to(1)})

    def gram_second(p):
        return gram_copy(
            1, gram.at[core, side, 0], gram.at[core, side, p], {"leaf": to(2 * p)}
        )

    def gram_third():
        return gram_copy(2, gram.at[core, side], gram.at[core, side], {"leaf": to(1)})

    def gram_fourth():
        return gram_copy(3, gram.at[core], gram.at[core], {"probe": 1 - core})

    def gram_others():
        return gram.at[core, side, pl.ds(1, n // 2 - 1)]

    if fused:
        square = dot(basis_ref[:upper, :], basis_ref[:upper, :], NT)
        first = square[:K, :]
        second = jnp.concatenate([square[K : 2 * K, K:], square[2 * K :, 2 * K :]], axis=1)
        for h, block in enumerate((first, second)):
            tail = jnp.concatenate([block[: K // 2, 128:], block[K // 2 :, 128:]], axis=1)
            packed = jnp.concatenate([block[:, :128], tail], axis=0)
            gram_own[h, 0] = packed[:48]
            gram_own[h, 1] = packed[48:]
        gram_first().start()

    def build_forms():
        pairs = []
        for p in range(n // 2):
            rows_of = []
            for h in range(2):
                packed = jnp.concatenate([gram[h, 0, p], gram[h, 1, p]], axis=0)
                tail = jnp.concatenate([packed[K:, :K], packed[K:, K:]], axis=0)
                rows_of.append(jnp.concatenate([packed[:K], tail], axis=1))
            pairs.append(rows_of)
        top = functools.reduce(jnp.maximum, [jnp.abs(block) for blocks in pairs for block in blocks])
        top = jnp.max(jnp.max(top, axis=1, keepdims=True), axis=0, keepdims=True)
        top = jnp.maximum(top, 1e-30)
        turn = 1.0 / top
        lane_k = lax.broadcasted_iota(jnp.int32, (K, upper), 1)
        for p, (a, b) in enumerate(pairs):
            none = jnp.zeros((K, K), F32)
            grid = [
                jnp.where(lane_k < K, a, 2.0 * a),
                jnp.concatenate([none, b[:, :K], 2.0 * b[:, K : 2 * K]], axis=1),
                jnp.concatenate([none, none, b[:, 2 * K :]], axis=1),
            ]
            whole = jnp.concatenate(grid, axis=0) * turn
            hi = whole.astype(BF16)
            rest = whole - hi.astype(F32)
            mid = rest.astype(BF16)
            low = (rest - mid.astype(F32)).astype(BF16)
            forms[p, 0] = hi
            forms[p, 1] = mid
            forms[p, 2] = low
        return top

    loads[3].wait()
    factor = ROOT_THREE / scale_ref[0]
    for t in range(count):
        cols = slice(t * LEAF, (t + 1) * LEAF)
        coords = points_ref[:, cols] * factor
        tall = jnp.transpose(
            jnp.concatenate([coords, jnp.zeros((5, LEAF), F32)], axis=0)
        )
        for c in range(LEAF // CHUNK):
            part = slice(c * CHUNK, (c + 1) * CHUNK)
            square = None
            for axis in range(3):
                offset = tall[part, axis : axis + 1] - coords[axis : axis + 1, :]
                term = offset * offset
                square = term if square is None else square + term
            scaled = square * lax.rsqrt(jnp.maximum(square, 1e-30))
            tiles[t, part, :] = ((1.0 + scaled) * jnp.exp(-scaled)).astype(BF16)

    if fused:
        gram_first().wait_recv()
        gram[core, side, 0] = gram_own[core, side] + gram_inbox[...]
        for p in range(1, n // 2):
            gram_second(p).start()

    lane = lax.broadcasted_iota(jnp.int32, (rows, width), 1)
    halves = 2 ** (total - cross - 1)
    half = span // halves
    lane128 = lax.broadcasted_iota(jnp.int32, (rows, 128), 1)

    iterate = jnp.zeros_like(right)
    remain = right
    direction = right
    norm_now = None
    for it in range(ITERS):
        if fused and it == 1:
            gram_third().wait_recv()
            gram_fourth().start()
        near = jnp.concatenate(
            [dot(low16[:, t * LEAF : (t + 1) * LEAF], tiles[t]) for t in range(count)], axis=1
        )
        local = [
            dot(low16[:, h * half : (h + 1) * half], basis_ref[upper:, h * half : (h + 1) * half], NT)
            for h in range(halves)
        ]
        spread = []
        for h in range(halves):
            cuts = []
            for depth in range(total - cross):
                size = halves // 2**depth
                first = h // size * size
                whole = local[first]
                for other in range(first + 1, first + size):
                    whole = whole + local[other]
                cuts.append(whole[:, depth * K : (depth + 1) * K])
            node = jnp.concatenate(cuts, axis=1).astype(BF16)
            spread.append(dot(node, basis_ref[upper:, h * half : (h + 1) * half]))
        result = near + NOISE * direction + jnp.concatenate(spread, axis=1)
        mine = jnp.sum(direction * result, axis=1, keepdims=True)
        more = it + 1 < ITERS
        whole_first = fused and it == 0
        if whole_first:
            pass
        elif fused:
            parts = [mine, jnp.sum(remain * remain, axis=1, keepdims=True)]
            message = jnp.zeros((rows, width), F32)
            if more:
                unit = result * shrink
                wide = unit.astype(BF16).astype(F32)
                both = jnp.concatenate([wide, unit - wide], axis=0).astype(BF16)
                seen = dot(both, basis_ref[:upper, :], NT)
                seen = seen[:rows] + seen[rows:]
                message = jnp.concatenate([seen, jnp.zeros((rows, width - upper), F32)], axis=1)
                parts += [
                    jnp.sum(unit * unit, axis=1, keepdims=True),
                    jnp.sum(remain * result, axis=1, keepdims=True),
                ]
            for i, part in enumerate(parts):
                message = jnp.where(lane == upper + i, part, message)
            scalars[it, 0] = message
        elif it == 0:
            first_norm = jnp.sum(remain * remain, axis=1, keepdims=True)
            scalars[it, 0] = jnp.where(lane128 < 64, mine, first_norm)
        else:
            scalars[it, 0] = jnp.broadcast_to(mine, (rows, 128))
        if not whole_first:
            broadcast(scalars, it, ITERS + it)

        arrived(sums, it, it)
        levels = tree_levels([sums[it, j] for j in range(n)])
        node = jnp.zeros((rows, width), F32)
        cover = jnp.zeros((rows, width), F32)
        for depth in range(cross):
            here = (lane >= depth * K) & (lane < (depth + 1) * K)
            nodes = levels[cross - depth]
            node = jnp.where(here, nodes[0][:rows], node)
            terms = [s[:rows].astype(BF16).astype(F32) * (s[:rows] + s[rows:]) for s in nodes]
            cover = jnp.where(here, tree_levels(terms)[-1][0], cover)
        result = result + dot(node[:, :upper].astype(BF16), basis_ref[:upper, :])
        cover = jnp.sum(cover, axis=1, keepdims=True)
        if whole_first:
            size = jnp.maximum(jnp.max(jnp.abs(result), axis=1, keepdims=True), 1e-30)
            shrink = 1.0 / size
            unit = result * shrink
            message = jnp.zeros((rows, width), F32)
            for i, part in enumerate(
                [
                    jnp.sum(direction * result, axis=1, keepdims=True),
                    jnp.sum(remain * remain, axis=1, keepdims=True),
                    jnp.sum(unit * unit, axis=1, keepdims=True),
                    size,
                ]
            ):
                message = jnp.where(lane == upper + i, part, message)
            scalars[it, 0] = message
            broadcast(scalars, it, ITERS + it)
            others = gram_others()
            pltpu.make_async_copy(others, others, recv_sem.at[2 * ITERS + 1]).wait()
            gram_third().start()

        if fused:
            if more:
                chains, turned = [], []
                for p in range(n // 2):
                    chain = jnp.zeros((rows, width), F32)
                    full = jnp.zeros((rows, width), F32)
                    for depth in range(cross):
                        here = (lane >= depth * K) & (lane < (depth + 1) * K)
                        at = levels[cross - depth][p // 2 ** (cross - 1 - depth)]
                        chain = jnp.where(here, at[:rows].astype(BF16).astype(F32), chain)
                        if p % 2 ** (cross - 1 - depth) == 0:
                            full = jnp.where(here, at[:rows] + at[rows:], full)
                    chains.append(chain)
                    turned.append(full)
                if it > 0:
                    moved = [now - ratio * old for now, old in zip(turned, turned_old)]
                    terms = [chain * there for chain, there in zip(chains, moved)]
                    remain_cover = jnp.sum(tree_levels(terms)[-1][0], axis=1, keepdims=True)
                turned_old = turned
                if it == 1:
                    gram_fourth().wait_recv()
                    form_top = build_forms()
                if it > 0:
                    terms = []
                    for p in range(n // 2):
                        chain16 = chains[p][:, :upper].astype(BF16)
                        image = dot(chain16, forms[p, 0]) + (
                            dot(chain16, forms[p, 1]) + dot(chain16, forms[p, 2])
                        )
                        terms.append(image * chains[p][:, :upper])
                    form = jnp.sum(tree_levels(terms)[-1][0], axis=1, keepdims=True)

            arrived(scalars, it, ITERS + it)
            got = [scalars[it, j] for j in range(n)]
            gathered = tree_levels(got)[-1][0]
            curve = gathered[:, upper : upper + 1]
            if it > 0:
                curve = curve + cover
            norm_now = gathered[:, upper + 1 : upper + 2]
            alpha = norm_now / curve
            if more and it == 0:
                sizes = [row[:, upper + 3 : upper + 4] for row in got]
                terms = []
                for j in range(n):
                    reach = alpha * sizes[j]
                    terms.append(reach * (reach * got[j][:, upper + 2 : upper + 3]))
                spent = tree_levels(terms)[-1][0]
                norm_next = (norm_now - 2.0 * (alpha * curve)) + spent
                ratio = norm_next / norm_now
            elif more:
                terms = []
                for j in range(n):
                    reach = alpha * sizes[j]
                    factors = jnp.where(
                        lane < upper,
                        (2.0 * alpha) * chains[j // 2],
                        jnp.where(lane == upper + 2, reach, 0.0),
                    )
                    terms.append(reach * (factors * got[j]))
                spent = jnp.sum(tree_levels(terms)[-1][0], axis=1, keepdims=True)
                crossed = alpha * (gathered[:, upper + 3 : upper + 4] + remain_cover)
                norm_next = (norm_now - 2.0 * crossed) + (spent + (alpha * form_top) * (alpha * form))
                ratio = norm_next / norm_now
            iterate = iterate + alpha * direction
            remain = remain - alpha * result
            if more:
                direction = remain + ratio * direction
                low16 = project_and_send(direction, it + 1)
            continue

        arrived(scalars, it, ITERS + it)
        gathered = tree_levels([scalars[it, j] for j in range(n)])[-1][0]
        curve = gathered[:, :1] + cover
        if it == 0:
            norm_now = gathered[:, 64:65]
        alpha = norm_now / curve
        remain = remain - alpha * result
        if it + 1 < ITERS:
            at = ITERS + it
            scalars[at, 0] = jnp.broadcast_to(
                jnp.sum(remain * remain, axis=1, keepdims=True), (rows, 128)
            )
            broadcast(scalars, at, ITERS + at)
            iterate = iterate + alpha * direction
            arrived(scalars, at, ITERS + at)
            norm_next = tree_levels([scalars[at, j] for j in range(n)])[-1][0][:, :1]
            direction = remain + norm_next / norm_now * direction
            norm_now = norm_next
            low16 = project_and_send(direction, it + 1)
        else:
            iterate = iterate + alpha * direction

    for t in range(count):
        cols = slice(t * LEAF, (t + 1) * LEAF)
        both = jnp.concatenate([iterate[:, cols], remain[:, cols]], axis=0)
        placed = join3(dot(split3(both), picks[t], NT))
        both_ref[:, cols] = placed
    for it in range(ITERS):
        left(sums, it, it)
    for at in range(ITERS if fused else 2 * ITERS - 1):
        left(scalars, at, ITERS + at)
    if fused:
        gram_first().wait_send()
        others = gram_others()
        pltpu.make_async_copy(others, others, send_sem.at[2 * ITERS + 1]).wait()
        gram_third().wait_send()
        gram_fourth().wait_send()


def body(rhs, points, basis, tree_order, lengthscale):
    rows, span = rhs.shape
    n = lax.axis_size("leaf")
    cross = n.bit_length() - 1
    total = basis.shape[0] // K
    fused = n == 8
    width = -(-(cross * K + 64) // 128) * 128
    vmem = pl.BlockSpec(memory_space=pltpu.VMEM)
    hbm = pl.BlockSpec(memory_space=pltpu.MemorySpace.HBM)
    rounds = 3 * ITERS

    def kernel(*refs):
        if not fused:
            refs = refs[:10] + (None,) * 4 + refs[10:]
        cg_kernel(n, cross, total, *refs)

    both = pl.pallas_call(
        kernel,
        out_shape=pltpu.VMEM((2 * rows, span), F32),
        in_specs=[hbm, hbm, hbm, hbm, pl.BlockSpec(memory_space=pltpu.SMEM)],
        out_specs=vmem,
        scratch_shapes=[shape for shape in [
            pltpu.VMEM((span // LEAF, LEAF, LEAF), BF16),
            pltpu.VMEM((span // LEAF, LEAF, LEAF), BF16),
            pltpu.VMEM((ITERS, n, 2 * rows, width), F32),
            pltpu.VMEM((ITERS, n, rows, width) if fused else (2 * ITERS - 1, n, rows, 128), F32),
            pltpu.VMEM((2, 2, n // 2, K * 3 // 4, 128), F32) if fused else None,
            pltpu.VMEM((2, 2, K * 3 // 4, 128), F32) if fused else None,
            pltpu.VMEM((K * 3 // 4, 128), F32) if fused else None,
            pltpu.VMEM((n // 2, 3, cross * K, cross * K), BF16) if fused else None,
            pltpu.VMEM((rows, span), F32),
            pltpu.VMEM((3, span), F32),
            pltpu.VMEM(basis.shape, BF16),
            pltpu.VMEM((1, span), jnp.int32),
            pltpu.SemaphoreType.DMA((rounds,)),
            pltpu.SemaphoreType.DMA((rounds,)),
            pltpu.SemaphoreType.DMA((4,)),
        ] if shape is not None],
        compiler_params=pltpu.CompilerParams(
            collective_id=0, has_side_effects=True, vmem_limit_bytes=63 * 2**20
        ),
        name="cg",
    )(rhs, points, basis, tree_order.reshape(1, span), lengthscale)
    return both[:rows], both[rows:]


def solution(mesh):
    in_specs = (
        P("probe", ("groups", "leaf")),
        P(None, ("groups", "leaf")),
        P(None, ("groups", "leaf")),
        P(("groups", "leaf")),
        P("groups"),
    )
    out_specs = (P("probe", ("groups", "leaf")), P("probe", ("groups", "leaf")))
    return jax.shard_map(body, mesh=mesh, in_specs=in_specs, out_specs=out_specs, check_vma=False)
```
